1024 devices in a mesh: mesh: 32 (over y, x), sub: 32 (over z, core).
Axes of the slice: x: 4, y: 8, z: 16, core: 2. Of those that a mesh axis runs over, the one named last changes fastest.
Arguments:
- displacement: float32 [3, 2, 256, 4096], P(None, None, 'mesh', 'sub'), may hold values from -4 to 4
- velocity: float32 [3, 2, 256, 4096], P(None, None, 'mesh', 'sub'), may hold values from -6 to 6
- node_mass: float32 [2, 256, 4096], P(None, 'mesh', 'sub'), may hold values from 0.5 to 2
- moduli: float32 [2, 256, 4096], P(None, 'mesh', 'sub'), may hold values from 0.5 to 2
- stiffness: float32 [24, 24], replicated, may hold values from -0.45 to 12, as said below
- surface_ref: float32 [3, 256, 4096], P(None, 'mesh', 'sub'), may hold values from -6 to 6
- facets: float32 [32, 32, 6, 1024], P('mesh', 'sub'), may hold values from -6 to 6
- penalty: float32 [32, 32, 1024], P('mesh', 'sub'), may hold values from 0.5 to 4
- owners: int32 [2, 32, 32, 8, 1], P(None, 'mesh', 'sub'), may hold values from 0 to 31; in each aligned block of 8 rows (0 to 7, 8 to 15, ..., all dimensions but the last counted through in order) at most 2 rows name the same one
- facet_pairs: int32 [2, 256, 4096], P(None, 'mesh', 'sub'), may hold values from 0 to 1023
Outputs:
- final_displacement: float32 [3, 2, 256, 4096], P(None, None, 'mesh', 'sub')
- final_velocity: float32 [3, 2, 256, 4096], P(None, None, 'mesh', 'sub')
The draws below stay inside these ranges and needn't reach their ends.
Inputs may be any that keep to these rules, and one draw needn't show every extreme that they name: `owners`: in every step no device sends more than 2 of its blocks to one owner, and some device sends exactly 2 to one owner. `stiffness`: Symmetric.
All inputs are finite; a program needn't handle non-finite values.
Results may differ from the reference program's by a relative error of at most 0.0001.
Values sent between devices are 32-bit elements; how exact they have to be, the bound alone decides.
No kernel may reach another device: no remote copies, remote signals or barrier semaphores. Data moves between devices by JAX's collectives and lax.ppermute only.
A program may use at most 64 MiB of HBM per device.

```python
import math
import jax
import jax.numpy as jnp
import numpy as np
from jax import lax

NZ = 2
BLOCK = 128
TF = 1024
STEPS = 2
OWNERS = 32
SUBPARTS = 32
SB = 8
CAP = 2
NX = 256
NY = 4096
N_MESH = 32


def draw_stiffness(key, part):
    key_off = jax.random.fold_in(key, 11)
    key_diag = jax.random.fold_in(key, 12)
    sampled = jax.random.truncated_normal(key_off, -3.0, 3.0, (24, 24), jnp.float32) * 0.15
    symmetric = (sampled + sampled.T) * 0.5
    off_diagonal = symmetric * (1.0 - jnp.eye(24, dtype=jnp.float32))
    surplus = jax.random.uniform(key_diag, (24,), jnp.float32, 0.5, 1.5)
    return off_diagonal + jnp.diag(jnp.sum(jnp.abs(off_diagonal), axis=1) + surplus)


def touch_ends(entries, own_key, least, high):
    shape = entries.shape
    index_at = [jax.random.randint(jax.random.fold_in(own_key, axis), (), 0, shape[axis]) for axis in range(len(shape))]
    entries = entries.at[tuple(index_at)].set(least)
    longest = shape.index(max(shape))
    index_at[longest] = (index_at[longest] + 1) % shape[longest]
    return entries.at[tuple(index_at)].set(high)


def steps_of(rng, dims, cuts, least, high):
    def one(position, shards_of):
        draws = jax.random.uniform(jax.random.fold_in(jax.random.fold_in(rng, 6), position), (shards_of,), jnp.float32, least / len(cuts), high / len(cuts))
        return jnp.repeat(jnp.exp(draws), dims[position] // shards_of).reshape((-1,) + (1,) * (len(dims) - position - 1))

    gain = one(*cuts[0])
    for cut in cuts[1:]:
        gain = gain * one(*cut)
    return gain


def assign_block(stream_key, own, number, rows, number_of, top, reach, slope):
    order = jax.random.permutation(stream_key, number_of)
    heavy_load, usual = shares(number_of, rows * top, reach, slope, True), shares(number_of, rows * top, reach, slope, False)
    places = jnp.arange(number_of)

    def named(tallies, offset_by):
        used = int((tallies > 0).sum())
        fixed = max(1, used // 4)
        moved = fixed + (places - fixed + offset_by * (used - fixed)) % max(1, number_of - fixed)
        return jnp.zeros((number_of,), jnp.int32).at[order[jnp.where(places < fixed, places, moved)]].set(jnp.asarray(tallies, jnp.int32))

    tallies = jnp.where(number % 4 == 0, named(heavy_load, number // 4), named(usual, number - number // 4 - 1))
    mixed = jax.random.permutation(jax.random.fold_in(own, 3), number_of)
    source_of, taker = mixed[0:number_of // 2 * 2:2], mixed[1:number_of // 2 * 2:2]
    margin = jnp.minimum(tallies[source_of] - 1, reach - tallies[taker]) // 2
    margin = jnp.where((source_of == order[0]) | (taker == order[0]) | (tallies[taker] == 0), 0, jnp.maximum(margin, 0))
    moved = jax.random.randint(jax.random.fold_in(own, 4), (number_of // 2,), 0, 1 << 20) % (margin + 1)
    tallies = tallies.at[source_of].add(-moved).at[taker].add(moved)
    labels = jnp.searchsorted(jnp.cumsum(tallies), jnp.arange(rows * top), side="right").astype(jnp.int32)
    listing = labels.reshape(top, rows).T
    listing = listing[jax.random.permutation(jax.random.fold_in(own, 1), rows)]
    offset_by = jax.random.randint(jax.random.fold_in(own, 2), (rows, 1), 0, top)
    return jnp.take_along_axis(listing, (jnp.arange(top)[None, :] + offset_by) % top, axis=1)


def shares(amount, total, reach, lean, full):
    portions = [(1 << 20) // math.isqrt(rank ** lean) + 1 for rank in range(1, amount + 1)]
    largest = reach if full else min(reach, max(-(-total // amount), total * portions[0] // sum(portions)))
    least = 1 if total - largest >= amount - 1 else 0
    given, spare = [largest] + [least] * (amount - 1), total - largest - least * (amount - 1)
    while spare > 0:
        free = [i for i in range(1, amount) if given[i] < largest] or [i for i in range(1, amount) if given[i] < reach]
        whole, remaining = sum([portions[i] for i in free]), spare
        for i in free:
            more = min(reach - given[i], max(1, remaining * portions[i] // whole), spare)
            given[i] = given[i] + more
            spare = spare - more
    return np.array(given)


def bell_draw(rng, shape, width, bound, cuts=(), held_as=jnp.bfloat16):
    array = width * jax.random.normal(rng, shape, jnp.float32)
    if cuts:
        array = array * steps_of(rng, shape, cuts, -0.22, 0.18)
    return jnp.clip(array, -bound, bound).astype(held_as)


def setup_inputs(seed: int = 0) -> dict:
    arg_keys = jax.random.split(jax.random.key(seed), 11)
    displacement = bell_draw(arg_keys[0], (3, NZ, NX, NY), 0.3, 4.0, ((2, 32), (3, 32)), jnp.float32)
    velocity = bell_draw(arg_keys[1], (3, NZ, NX, NY), 1.0, 6.0, ((2, 32), (3, 32)), jnp.float32)
    node_mass = jnp.clip(jnp.exp(math.log(2.0) - 1.3862944 * jax.random.uniform(arg_keys[2], (NZ, NX, NY), jnp.float32) ** steps_of(arg_keys[2], (NZ, NX, NY), ((1, 32), (2, 32)), -0.2, 0.2)), 0.5, 2.0)
    moduli = jnp.clip(jnp.exp(math.log(2.0) - 1.3862944 * jax.random.uniform(arg_keys[3], (NZ, NX, NY), jnp.float32) ** steps_of(arg_keys[3], (NZ, NX, NY), ((1, 32), (2, 32)), -0.2, 0.2)), 0.5, 2.0)
    stiffness = draw_stiffness(jax.random.fold_in(arg_keys[10], 71), 0)
    surface_ref = bell_draw(arg_keys[5], (3, NX, NY), 1.0, 6.0, ((1, 32), (2, 32)), jnp.float32)
    facets = bell_draw(arg_keys[6], (OWNERS, SUBPARTS, 6, TF), 1.0, 6.0, ((0, 32), (1, 32)), jnp.float32)
    penalty = jnp.clip(jnp.exp(math.log(4.0) - 2.0794415 * jax.random.uniform(arg_keys[7], (OWNERS, SUBPARTS, TF), jnp.float32) ** steps_of(arg_keys[7], (OWNERS, SUBPARTS, TF), ((0, 32), (1, 32)), -0.2, 0.2)), 0.5, 4.0)
    owners_keys = jax.random.split(jax.random.fold_in(arg_keys[8], 1), STEPS * OWNERS * SUBPARTS * SB // SB)
    owners_turns = jax.random.permutation(jax.random.fold_in(arg_keys[8], 3), STEPS * OWNERS * SUBPARTS * SB // SB)
    owners = jax.vmap(lambda own, number: assign_block(jax.random.fold_in(arg_keys[8], 2), own, number, SB, OWNERS, 1, CAP, 2))(owners_keys, owners_turns).reshape((STEPS, OWNERS, SUBPARTS, SB, 1))
    facet_pairs = touch_ends(jax.random.randint(arg_keys[9], (STEPS, NX, NY), 0, TF), jax.random.fold_in(arg_keys[9], 1), 0, TF - 1).astype(jnp.int32)
    return dict(displacement=displacement, velocity=velocity, node_mass=node_mass, moduli=moduli, stiffness=stiffness, surface_ref=surface_ref, facets=facets, penalty=penalty, owners=owners, facet_pairs=facet_pairs)


TIME_STEP = 0.1
CORNER_SHIFTS = ((0, 0, 0), (0, 0, 1), (0, 1, 0), (0, 1, 1), (1, 0, 0), (1, 0, 1), (1, 1, 0), (1, 1, 1))


def node_forces(node_patch, patch_moduli, stiffness):
    layers = node_patch.shape[1]
    row_count = node_patch.shape[2] - 2
    col_count = node_patch.shape[3] - 2
    element_scale = jnp.zeros((layers - 1, row_count + 1, col_count + 1), jnp.float32)
    corners = []
    for shift_z, shift_x, shift_y in CORNER_SHIFTS:
        element_scale = element_scale + patch_moduli[shift_z:shift_z + layers - 1, shift_x:shift_x + row_count + 1, shift_y:shift_y + col_count + 1]
        corners.append(node_patch[:, shift_z:shift_z + layers - 1, shift_x:shift_x + row_count + 1, shift_y:shift_y + col_count + 1])
    element_scale = element_scale * 0.125
    stacked = jnp.concatenate(corners, axis=0).reshape(24, -1)
    forces = jnp.dot(stiffness, stacked, precision=lax.Precision.HIGHEST).reshape(24, layers - 1, row_count + 1, col_count + 1) * element_scale[None]
    summed = jnp.zeros((3, layers, row_count, col_count), jnp.float32)
    for corner, (shift_z, shift_x, shift_y) in enumerate(CORNER_SHIFTS):
        contribution = forces[3 * corner:3 * corner + 3, :, 1 - shift_x:1 - shift_x + row_count, 1 - shift_y:1 - shift_y + col_count]
        summed = summed.at[:, shift_z:shift_z + layers - 1].add(contribution)
    return summed


def contact_push(points, facet_rows, stiffness_row):
    normal_gap = jnp.sum(facet_rows[3:6] * (points - facet_rows[0:3]), axis=0)
    return facet_rows[3:6] * (stiffness_row * jnp.maximum(-normal_gap, 0.0))[None]


def internal_forces(displacement, moduli, stiffness):
    padded = jnp.pad(displacement, ((0, 0), (0, 0), (1, 1), (1, 1)), mode="wrap")
    padded_moduli = jnp.pad(moduli, ((0, 0), (1, 1), (1, 1)), mode="wrap")
    row_count = displacement.shape[2] // N_MESH

    def one_block(block_index):
        row_start = block_index * row_count
        node_patch = lax.dynamic_slice_in_dim(padded, row_start, row_count + 2, 2)
        patch_moduli = lax.dynamic_slice_in_dim(padded_moduli, row_start, row_count + 2, 1)
        return node_forces(node_patch, patch_moduli, stiffness)

    pieces = lax.map(one_block, jnp.arange(N_MESH, dtype=jnp.int32))
    return pieces.transpose(1, 2, 0, 3, 4).reshape(displacement.shape)


def contact_forces(positions, owner_step, pair_step, facets, penalty):
    groups = facets.shape[0]
    sub_count = facets.shape[1]
    table_width = facets.shape[3]
    row_count = positions.shape[1] // groups
    col_count = positions.shape[2] // sub_count
    points = positions.reshape(3, groups, row_count, sub_count, col_count).transpose(0, 1, 3, 2, 4).reshape(3, -1)
    pair_rows = pair_step.reshape(groups, row_count, sub_count, col_count).transpose(0, 2, 1, 3).reshape(groups, sub_count, -1)
    per_point = jnp.repeat(owner_step[..., 0], BLOCK, axis=2)
    sub_index = jnp.arange(sub_count, dtype=jnp.int32)[None, :, None]
    flat_index = ((per_point * sub_count + sub_index) * table_width + pair_rows).reshape(-1).astype(jnp.int32)
    whole_table = facets.transpose(2, 0, 1, 3).reshape(6, -1)
    facet_rows = jnp.take(whole_table, flat_index, axis=1)
    pushed = contact_push(points, facet_rows, jnp.take(penalty.reshape(-1), flat_index))
    return pushed.reshape(3, groups, sub_count, row_count, col_count).transpose(0, 1, 3, 2, 4).reshape(positions.shape)


def reference(displacement, velocity, node_mass, moduli, stiffness, surface_ref, facets, penalty, owners, facet_pairs):
    for step_index in range(STEPS):
        internal = internal_forces(displacement, moduli, stiffness)
        pushed = contact_forces(surface_ref + displacement[:, 0], owners[step_index], facet_pairs[step_index], facets, penalty)
        net_force = (-internal).at[:, 0].add(pushed)
        velocity = velocity + TIME_STEP * net_force / node_mass[None]
        displacement = displacement + TIME_STEP * velocity
    return displacement, velocity
```

```python
import jax
import jax.numpy as jnp
from jax import lax
from jax.experimental import pallas as pl
from jax.experimental.pallas import tpu as pltpu
from jax.sharding import PartitionSpec as P

DT = 0.1
F32 = jnp.float32
VMEM = pl.BlockSpec(memory_space=pltpu.VMEM)
SMEM = pl.BlockSpec(memory_space=pltpu.SMEM)
ROWS = 8
COLS = 128
OWNERS = 32
AT_U, AT_E, AT_V, AT_M, AT_X, AT_P, AT_O = 0, 12, 16, 22, 24, 27, 28
MSG = 32


def struct(*shape, dtype=F32):
    return jax.ShapeDtypeStruct(shape, dtype)


def lanes(shape):
    return lax.broadcasted_iota(jnp.int32, shape, len(shape) - 1)


def pack_kernel(u, v, mass, mod, ref, fac, pen, own, pair, table, up, down):
    root = jnp.sqrt(pen[...])
    n = [fac[3 + m : 4 + m, :] for m in range(3)]
    c = [fac[m : m + 1, :] for m in range(3)]
    dist = n[0] * c[0] + n[1] * c[1] + n[2] * c[2]
    rows = [root * n[0], root * n[1], root * n[2], root * dist]
    half = fac.shape[1] // 2
    mine = jnp.concatenate([r[:, :half] for r in rows] + [r[:, half:] for r in rows], axis=0)
    for o in range(OWNERS):
        table[o] = mine
    for out, two, one in ((down, ROWS - 2, ROWS - 1), (up, 0, 0)):
        for m in range(3):
            for k in range(2):
                ch = 2 * m + k
                out[AT_U + 2 * ch : AT_U + 2 * ch + 2, :] = u[m, k, two : two + 2, :]
                out[AT_V + ch : AT_V + ch + 1, :] = v[m, k, one : one + 1, :]
            out[AT_X + m : AT_X + m + 1, :] = ref[m, one : one + 1, :]
        for k in range(2):
            out[AT_E + 2 * k : AT_E + 2 * k + 2, :] = mod[k, two : two + 2, :]
            out[AT_M + k : AT_M + k + 1, :] = mass[k, one : one + 1, :]
        out[AT_P : AT_P + 1, :] = pair[0, one : one + 1, :].astype(F32)
        out[AT_O : AT_O + 1, :] = jnp.full((1, COLS), own[0, 0, 0, one, 0]).astype(F32)
        out[AT_O + 1 :, :] = jnp.zeros((MSG - AT_O - 1, COLS), F32)


def extend_kernel(u, mod, above, below, ext, left, right):
    for ch in range(8):
        at = AT_U + 2 * ch if ch < 6 else AT_E + 2 * (ch - 6)
        own = u[ch // 2, ch % 2] if ch < 6 else mod[ch - 6]
        ext[16 * ch : 16 * ch + 2, :] = above[at : at + 2, :]
        ext[16 * ch + 2 : 16 * ch + 10, :] = own
        ext[16 * ch + 10 : 16 * ch + 12, :] = below[at : at + 2, :]
        ext[16 * ch + 12 : 16 * ch + 16, :] = jnp.zeros((4, COLS), F32)
    turned = jnp.transpose(ext[...])
    left[...] = turned[0:1, :]
    right[...] = turned[COLS - 1 : COLS, :]


def edge_columns(from_left, from_right):
    sub = lax.broadcasted_iota(jnp.int32, (128, COLS), 0)
    both = jnp.where(sub < 64, jnp.broadcast_to(from_left, (128, COLS)), jnp.broadcast_to(from_right, (128, COLS)))
    return jnp.transpose(both)


def with_columns(here, edges):
    lane = lanes(here.shape)
    return jnp.where(lane == COLS - 1, edges, pltpu.roll(here, COLS - 1, axis=1))


def internal_tile(stiff, at_left, at_right, at_edge, scale, at, scale_at):
    lane0 = lanes((ROWS, COLS)) == 0
    straight, moved, edge = {}, {}, {}
    for i in range(2):
        start = at + 1 - i
        rows = [pl.ds(start + x, ROWS) for x in range(2)]
        lefts = [at_left[ch, rows[x], :] for ch in range(6) for x in range(2)]
        rights = [at_right[ch, rows[x], :] for ch in range(6) for x in range(2)]
        edges = [at_edge[ch, rows[x], :] for ch in range(6) for x in range(2)]
        s_main = scale[0, pl.ds(start + scale_at, ROWS), :]
        s_edge = scale[1, pl.ds(start + scale_at, ROWS), :]
        for k in range(2):
            for m in range(3):
                for e in range(2):
                    row = 3 * (4 * k + 2 * i + e) + m
                    main = side = None
                    for kk in range(2):
                        for x in range(2):
                            for ee in range(2):
                                for mm in range(3):
                                    w = stiff[row, 3 * (4 * kk + 2 * x + ee) + mm]
                                    j = 2 * (2 * mm + kk) + x
                                    t = w * (rights if ee else lefts)[j]
                                    main = t if main is None else main + t
                                    if e:
                                        t = w * (lefts if ee else edges)[j]
                                        side = t if side is None else side + t
                    into = moved if e else straight
                    ch = 2 * m + k
                    main = main * s_main
                    into[ch] = main if i == 0 else into[ch] + main
                    if e:
                        side = side * s_edge
                        edge[ch] = side if i == 0 else edge[ch] + side
    return [straight[ch] + jnp.where(lane0, edge[ch], pltpu.roll(moved[ch], 1, axis=1)) for ch in range(6)]


def first_kernel(stiff, ext, from_left, from_right, above, below, v, mass, ref, pair, vel, dis, weight, point, index, scale, at_left, at_right, at_edge):
    edges = edge_columns(from_left[...], from_right[...])
    zero = jnp.zeros((8, COLS), F32)
    for ch in range(6):
        here, side = ext[16 * ch : 16 * ch + 16, :], edges[16 * ch : 16 * ch + 16, :]
        at_left[ch, 0:16, :] = here
        at_right[ch, 0:16, :] = with_columns(here, side)
        at_edge[ch, 0:16, :] = side
        for buf in (at_left, at_right, at_edge):
            buf[ch, 16:24, :] = zero
    here = ext[96:112, :] + ext[112:128, :]
    side = edges[96:112, :] + edges[112:128, :]
    right = with_columns(here, side)
    for n, both in enumerate((here + right, side + here)):
        scale[n, 0:16, :] = (both + pltpu.roll(both, 15, axis=0)) * 0.125
        scale[n, 16:24, :] = zero
    for k in range(2):
        weight[k, 0:1, :] = above[AT_M + k : AT_M + k + 1, :]
        weight[k, 1:9, :] = mass[k]
        weight[k, 9:10, :] = below[AT_M + k : AT_M + k + 1, :]
        weight[k, 10:16, :] = jnp.ones((6, COLS), F32)
        weight[k] = DT / weight[k]
    for ch in range(6):
        vel[ch, 0:1, :] = above[AT_V + ch : AT_V + ch + 1, :]
        vel[ch, 1:9, :] = v[ch // 2, ch % 2]
        vel[ch, 9:10, :] = below[AT_V + ch : AT_V + ch + 1, :]
        vel[ch, 10:16, :] = zero[:6]
    for m in range(3):
        point[m, 0:1, :] = above[AT_X + m : AT_X + m + 1, :]
        point[m, 1:9, :] = ref[m]
        point[m, 9:10, :] = below[AT_X + m : AT_X + m + 1, :]
        point[m, 10:16, :] = zero[:6]
        point[m] = point[m] + at_left[2 * m, 1:17, :]
    index[0:1, :] = above[AT_P : AT_P + 1, :].astype(jnp.int32)
    index[1:9, :] = pair[0]
    index[9:10, :] = below[AT_P : AT_P + 1, :].astype(jnp.int32)
    index[10:16, :] = jnp.zeros((6, COLS), jnp.int32)
    for at in (0, 8):
        forces = internal_tile(stiff, at_left, at_right, at_edge, scale, at, 0)
        for ch in range(6):
            new = vel[ch, at : at + 8, :] - weight[ch % 2, at : at + 8, :] * forces[ch]
            vel[ch, at : at + 8, :] = new
            dis[ch, at : at + 8, :] = at_left[ch, at + 1 : at + 9, :] + DT * new


def look_up(table, owner, index, row, out):
    which = jnp.broadcast_to(index, (8, COLS))
    place, part = which & 127, (which >> 7) & 3
    found = None
    for c in range(4):
        got = jnp.take_along_axis(table[owner, :, c * COLS : (c + 1) * COLS], place, axis=1)
        found = got if found is None else jnp.where(part == c, got, found)
    found = jnp.where(which[0:4] >= 512, found[4:8], found[0:4])
    for c in range(4):
        out[c, row : row + 1, :] = found[c : c + 1]


def contact(words, points):
    depth = jnp.maximum(words[3] - (words[0] * points[0] + words[1] * points[1] + words[2] * points[2]), 0.0)
    return [words[m] * depth for m in range(3)]


def contact_kernel(owner, table, index, pair, vel, dis, weight, point, ref, new_vel, new_dis, push, left, right, words, square):
    words[:, 8:16, :] = jnp.zeros((4, 8, COLS), F32)
    for b in range(ROWS + 2):
        look_up(table, owner[b], index[b : b + 1, :], b, words)
    pushes = contact([words[c] for c in range(4)], [point[m] for m in range(3)])
    for m in range(3):
        step = weight[0] * pushes[m]
        new_vel[2 * m] = (vel[2 * m] + step)[1:9]
        new_vel[2 * m + 1] = vel[2 * m + 1, 1:9, :]
        new_dis[2 * m] = dis[2 * m] + DT * step
        new_dis[2 * m + 1] = dis[2 * m + 1]
    for ch in range(6):
        square[16 * ch : 16 * ch + 16, :] = new_dis[ch]
    square[96:128, :] = jnp.zeros((32, COLS), F32)
    turned = jnp.transpose(square[...])
    left[...] = turned[0:1, :]
    right[...] = turned[COLS - 1 : COLS, :]
    for b in range(ROWS):
        look_up(table, owner[ROWS + 2 + b], pair[1, b : b + 1, :], b, words)
    pushes = contact([words[c, 0:8, :] for c in range(4)], [ref[m] + new_dis[2 * m, 1:9, :] for m in range(3)])
    for m in range(3):
        push[m] = pushes[m]


def second_kernel(stiff, dis, vel, push, mass, scale, from_left, from_right, out_dis, out_vel, at_left, at_right, at_edge):
    edges = edge_columns(from_left[...], from_right[...])
    for ch in range(6):
        here, side = dis[ch], edges[16 * ch : 16 * ch + 16, :]
        at_left[ch, 0:16, :] = here
        at_right[ch, 0:16, :] = with_columns(here, side)
        at_edge[ch, 0:16, :] = side
    forces = internal_tile(stiff, at_left, at_right, at_edge, scale, 0, 1)
    for m in range(3):
        for k in range(2):
            ch = 2 * m + k
            net = push[m] - forces[ch] if k == 0 else -forces[ch]
            new = vel[ch] + DT * net / mass[k]
            out_vel[m, k] = new
            out_dis[m, k] = at_left[ch, 1:9, :] + DT * new


def call(kernel, outs, specs, scratch=()):
    return pl.pallas_call(
        kernel,
        out_shape=outs,
        in_specs=specs,
        out_specs=jax.tree.map(lambda _: VMEM, outs),
        scratch_shapes=list(scratch),
        compiler_params=pltpu.CompilerParams(vmem_limit_bytes=16 * 1024 * 1024),
    )


def swapped(to_next, to_last, axis):
    size = lax.axis_size(axis)
    up = [(i, (i + 1) % size) for i in range(size)]
    down = [(j, i) for i, j in up]
    return lax.ppermute(to_next, axis, up), lax.ppermute(to_last, axis, down)


def shards(u, v, mass, mod, stiff, ref, facets, penalty, owners, pair):
    width = facets.shape[-1]
    buffers = [pltpu.VMEM((6, 24, COLS), F32)] * 3
    table, up, down = call(
        pack_kernel,
        (struct(OWNERS, 8, width // 2), struct(MSG, COLS), struct(MSG, COLS)),
        [VMEM] * 7 + [SMEM, VMEM],
    )(u, v, mass, mod, ref, facets.reshape(6, width), penalty.reshape(1, width), owners, pair)
    tables = lax.all_to_all(table, "mesh", split_axis=0, concat_axis=0, tiled=True)
    above, below = swapped(down, up, "mesh")
    ext, left, right = call(
        extend_kernel, (struct(128, COLS), struct(1, COLS), struct(1, COLS)), [VMEM] * 4
    )(u, mod, above, below)
    from_left, from_right = swapped(right, left, "sub")
    vel, dis, weight, point, index, scale = call(
        first_kernel,
        (
            struct(6, 16, COLS),
            struct(6, 16, COLS),
            struct(2, 16, COLS),
            struct(3, 16, COLS),
            struct(16, COLS, dtype=jnp.int32),
            struct(2, 24, COLS),
        ),
        [SMEM] + [VMEM] * 9,
        buffers,
    )(stiff, ext, from_left, from_right, above, below, v, mass, ref, pair)
    mine = owners.reshape(2, ROWS)
    outer = [side[AT_O, :1].astype(jnp.int32) for side in (above, below)]
    owner = jnp.concatenate([outer[0], mine[0], outer[1], mine[1]])
    new_vel, new_dis, push, left, right = call(
        contact_kernel,
        (
            struct(6, ROWS, COLS),
            struct(6, 16, COLS),
            struct(3, ROWS, COLS),
            struct(1, COLS),
            struct(1, COLS),
        ),
        [SMEM] + [VMEM] * 8,
        [pltpu.VMEM((4, 16, COLS), F32), pltpu.VMEM((128, COLS), F32)],
    )(owner, tables, index, pair, vel, dis, weight, point, ref)
    from_left, from_right = swapped(right, left, "sub")
    return call(
        second_kernel,
        (struct(3, 2, ROWS, COLS), struct(3, 2, ROWS, COLS)),
        [SMEM] + [VMEM] * 7,
        buffers,
    )(stiff, new_dis, new_vel, push, mass, scale, from_left, from_right)


def solution(mesh):
    in_specs = (
        P(None, None, "mesh", "sub"),
        P(None, None, "mesh", "sub"),
        P(None, "mesh", "sub"),
        P(None, "mesh", "sub"),
        P(),
        P(None, "mesh", "sub"),
        P("mesh", "sub", None, None),
        P("mesh", "sub", None),
        P(None, "mesh", "sub", None, None),
        P(None, "mesh", "sub"),
    )
    out_specs = (P(None, None, "mesh", "sub"), P(None, None, "mesh", "sub"))
    return jax.shard_map(shards, mesh=mesh, in_specs=in_specs, out_specs=out_specs, check_vma=False)
```

```python
import jax
import jax.numpy as jnp
from jax import lax
from jax.experimental import pallas as pl
from jax.experimental.pallas import tpu as pltpu
from jax.sharding import PartitionSpec as P

DT = 0.1
F32 = jnp.float32
VMEM = pl.BlockSpec(memory_space=pltpu.VMEM)
SMEM = pl.BlockSpec(memory_space=pltpu.SMEM)
ROWS = 8
COLS = 128
OWNERS = 32
AT_U, AT_E, AT_V, AT_M, AT_X, AT_P, AT_O = 0, 12, 16, 22, 24, 27, 28
MSG = 32


def struct(*shape, dtype=F32):
    return jax.ShapeDtypeStruct(shape, dtype)


def lanes(shape):
    return lax.broadcasted_iota(jnp.int32, shape, len(shape) - 1)


def pack_kernel(u, v, mass, mod, ref, fac, pen, pair, own, table, up, down, *held):
    arrays, sems = held[:-1], held[-1]
    copies = [pltpu.make_async_copy(a, b, sems.at[n]) for n, (a, b) in enumerate(zip((u, v, mass, mod, ref, fac, pen, pair), arrays))]
    for copy in copies:
        copy.start()
    for copy in copies:
        copy.wait()
    u, v, mass, mod, ref, fac, pen, pair = arrays
    root = jnp.sqrt(pen[...])
    c, n = [[fac[8 * (m + at) : 8 * (m + at) + 8, :] for m in range(3)] for at in (0, 3)]
    dist = n[0] * c[0] + n[1] * c[1] + n[2] * c[2]
    words = [root * n[0], root * n[1], root * n[2], root * dist]
    for q in range(4):
        mine = jnp.concatenate([w[4 * h + q : 4 * h + q + 1, :] for h in range(2) for w in words], axis=0)
        for o in range(OWNERS):
            table[o, 8 * q : 8 * q + 8, :] = mine
    for out, two, one in ((down, ROWS - 2, ROWS - 1), (up, 0, 0)):
        for m in range(3):
            for k in range(2):
                ch = 2 * m + k
                out[AT_U + 2 * ch : AT_U + 2 * ch + 2, :] = u[m, k, two : two + 2, :]
                out[AT_V + ch : AT_V + ch + 1, :] = v[m, k, one : one + 1, :]
            out[AT_X + m : AT_X + m + 1, :] = ref[m, one : one + 1, :]
        for k in range(2):
            out[AT_E + 2 * k : AT_E + 2 * k + 2, :] = mod[k, two : two + 2, :]
            out[AT_M + k : AT_M + k + 1, :] = mass[k, one : one + 1, :]
        out[AT_P : AT_P + 1, :] = pair[0, one : one + 1, :].astype(F32)
        out[AT_O : AT_O + 1, :] = jnp.full((1, COLS), own[0, 0, one]).astype(F32)
        out[AT_O + 1 :, :] = jnp.zeros((MSG - AT_O - 1, COLS), F32)


def extend_kernel(u, mod, above, below, ext, left, right):
    for ch in range(8):
        at = AT_U + 2 * ch if ch < 6 else AT_E + 2 * (ch - 6)
        own = u[ch // 2, ch % 2] if ch < 6 else mod[ch - 6]
        ext[16 * ch : 16 * ch + 2, :] = above[at : at + 2, :]
        ext[16 * ch + 2 : 16 * ch + 10, :] = own
        ext[16 * ch + 10 : 16 * ch + 12, :] = below[at : at + 2, :]
        ext[16 * ch + 12 : 16 * ch + 16, :] = jnp.zeros((4, COLS), F32)
    turned = jnp.transpose(ext[...])
    left[...] = turned[0:1, :]
    right[...] = turned[COLS - 1 : COLS, :]


def edge_columns(from_left, from_right):
    sub = lax.broadcasted_iota(jnp.int32, (128, COLS), 0)
    both = jnp.where(sub < 64, jnp.broadcast_to(from_left, (128, COLS)), jnp.broadcast_to(from_right, (128, COLS)))
    return jnp.transpose(both)


def with_columns(here, edges):
    lane = lanes(here.shape)
    return jnp.where(lane == COLS - 1, edges, pltpu.roll(here, COLS - 1, axis=1))


def corners():
    return [(3 * (4 * k + 2 * x + e) + m, 2 * m + k, x, e) for k in range(2) for x in range(2) for e in range(2) for m in range(3)]


def element_sums(weight, rows_of, sides, scales, at):
    total = {}
    for i in range(2):
        start = at + 1 - i
        values = {c: rows_of[e][ch, pl.ds(start + x, ROWS), :] for c, ch, x, e in corners()}
        for k in range(2):
            for m in range(3):
                force = None
                for c in range(24):
                    t = weight(k, i, m, c) * values[c]
                    force = t if force is None else force + t
                force = force * scales[pl.ds(start + sides, ROWS), :]
                total[2 * m + k] = force if i == 0 else total[2 * m + k] + force
    return [total[ch] for ch in range(6)]


def by_corner(stiff, e):
    return lambda k, i, m, c: stiff[3 * (4 * k + 2 * i + e) + m, c]


def first_kernel(stiff, owner, ext, from_left, from_right, above, below, v, mass, ref, pair, vel, dis, weight, point, index, who, scale, spread, at_left, at_right, at_edge):
    edges = edge_columns(from_left[...], from_right[...])
    zero = jnp.zeros((8, COLS), F32)
    lane = lanes((ROWS, COLS))
    for ch in range(6):
        here, side = ext[16 * ch : 16 * ch + 16, :], edges[16 * ch : 16 * ch + 16, :]
        at_left[ch, 0:16, :] = here
        at_right[ch, 0:16, :] = with_columns(here, side)
        at_edge[ch, 0:16, :] = side
        for buf in (at_left, at_right, at_edge):
            buf[ch, 16:24, :] = zero
    here = ext[96:112, :] + ext[112:128, :]
    side = edges[96:112, :] + edges[112:128, :]
    right = with_columns(here, side)
    for n, both in enumerate((here + right, side + here)):
        scale[n, 0:16, :] = (both + pltpu.roll(both, 15, axis=0)) * 0.125
        scale[n, 16:24, :] = zero
    for k in range(2):
        weight[k, 0:1, :] = above[AT_M + k : AT_M + k + 1, :]
        weight[k, 1:9, :] = mass[k]
        weight[k, 9:10, :] = below[AT_M + k : AT_M + k + 1, :]
        weight[k, 10:16, :] = jnp.ones((6, COLS), F32)
        weight[k] = DT / weight[k]
    for ch in range(6):
        vel[ch, 0:1, :] = above[AT_V + ch : AT_V + ch + 1, :]
        vel[ch, 1:9, :] = v[ch // 2, ch % 2]
        vel[ch, 9:10, :] = below[AT_V + ch : AT_V + ch + 1, :]
        vel[ch, 10:16, :] = zero[:6]
    for m in range(3):
        point[m, 0:1, :] = above[AT_X + m : AT_X + m + 1, :]
        point[m, 1:9, :] = ref[m]
        point[m, 9:10, :] = below[AT_X + m : AT_X + m + 1, :]
        point[m, 10:16, :] = zero[:6]
        point[m] = point[m] + at_left[2 * m, 1:17, :]
    index[0:1, :] = above[AT_P : AT_P + 1, :].astype(jnp.int32)
    index[1:9, :] = pair[0]
    index[9:10, :] = below[AT_P : AT_P + 1, :].astype(jnp.int32)
    index[10:16, :] = jnp.zeros((6, COLS), jnp.int32)
    who[0:1, :] = above[AT_O : AT_O + 1, :].astype(jnp.int32)
    who[9:10, :] = below[AT_O : AT_O + 1, :].astype(jnp.int32)
    for b in range(ROWS):
        who[1 + b : 2 + b, :] = jnp.full((1, COLS), owner[0, 0, b])
        who[16 + b : 17 + b, :] = jnp.full((1, COLS), owner[1, 0, b])
    who[10:16, :] = jnp.zeros((6, COLS), jnp.int32)
    for at in (0, 8):
        straight = element_sums(by_corner(stiff, 0), (at_left, at_right), 0, scale.at[0], at)
        moved = element_sums(by_corner(stiff, 1), (at_left, at_right), 0, scale.at[0], at)
        edge = element_sums(by_corner(stiff, 1), (at_edge, at_left), 0, scale.at[1], at)
        for ch in range(6):
            force = straight[ch] + jnp.where(lane == 0, edge[ch], pltpu.roll(moved[ch], 1, axis=1))
            new = vel[ch, at : at + 8, :] - weight[ch % 2, at : at + 8, :] * force
            vel[ch, at : at + 8, :] = new
            dis[ch, at : at + 8, :] = at_left[ch, at + 1 : at + 9, :] + DT * new
    row = lanes((1, COLS))
    for k in range(2):
        for i in range(2):
            for m in range(3):
                for c in range(24):
                    one, other = [stiff[3 * (4 * k + 2 * i + e) + m, c] for e in (1, 0)]
                    at = 24 * (6 * k + 3 * i + m) + c
                    spread[at : at + 1, :] = jnp.where(row < 64, one, other)
    scale[2] = jnp.where(lanes((24, COLS)) < 64, scale[1], scale[0])


def look_up(table, owner, index, row, out):
    which = jnp.broadcast_to(index, (8, COLS))
    place, part = which & 127, (which >> 7) & 3
    found = None
    for c in range(4):
        got = jnp.take_along_axis(table[owner, 8 * c : 8 * c + 8, :], place, axis=1)
        found = got if found is None else jnp.where(part == c, got, found)
    found = jnp.where(which[0:4] >= 512, found[4:8], found[0:4])
    for c in range(4):
        out[c, row : row + 1, :] = found[c : c + 1]


def contact(words, points):
    depth = jnp.maximum(words[3] - (words[0] * points[0] + words[1] * points[1] + words[2] * points[2]), 0.0)
    return [words[m] * depth for m in range(3)]


def contact_kernel(who, table, index, vel, dis, weight, point, new_vel, new_dis, left, right, words, square):
    words[:, 8:16, :] = jnp.zeros((4, 8, COLS), F32)
    for b in range(ROWS + 2):
        look_up(table, who[b, 0], index[b : b + 1, :], b, words)
    pushes = contact([words[c] for c in range(4)], [point[m] for m in range(3)])
    for m in range(3):
        step = weight[0] * pushes[m]
        new_vel[2 * m] = (vel[2 * m] + step)[1:9]
        new_vel[2 * m + 1] = vel[2 * m + 1, 1:9, :]
        new_dis[2 * m] = dis[2 * m] + DT * step
        new_dis[2 * m + 1] = dis[2 * m + 1]
    for ch in range(6):
        square[16 * ch : 16 * ch + 16, :] = new_dis[ch]
    square[96:128, :] = jnp.zeros((32, COLS), F32)
    turned = jnp.transpose(square[...])
    left[...] = turned[0:1, :]
    right[...] = turned[COLS - 1 : COLS, :]


def inner_kernel(who, stiff, table, pair, dis, vel, mass, ref, scale, base_dis, base_vel, weight, at_right, words):
    lane = lanes((ROWS, COLS))
    for b in range(ROWS):
        look_up(table, who[16 + b, 0], pair[1, b : b + 1, :], b, words)
    push = contact([words[c] for c in range(4)], [ref[m] + dis[2 * m, 1:9, :] for m in range(3)])
    for ch in range(6):
        at_right[ch] = pltpu.roll(dis[ch], COLS - 1, axis=1)
    straight = element_sums(by_corner(stiff, 0), (dis, at_right), 1, scale.at[0], 0)
    moved = element_sums(by_corner(stiff, 1), (dis, at_right), 1, scale.at[0], 0)
    for k in range(2):
        weight[k] = DT / mass[k]
        for m in range(3):
            ch = 2 * m + k
            force = jnp.where(lane == COLS - 1, 0.0, straight[ch]) + jnp.where(lane == 0, 0.0, pltpu.roll(moved[ch], 1, axis=1))
            net = push[m] - force if k == 0 else -force
            new = vel[ch] + weight[k] * net
            base_vel[ch] = new
            base_dis[ch] = dis[ch, 1:9, :] + DT * new


def outer_kernel(dis, base_dis, base_vel, weight, scale, spread, from_left, from_right, out_dis, out_vel, at_left, at_right):
    edges = edge_columns(from_left[...], from_right[...])
    lane = lanes((16, COLS))
    for ch in range(6):
        here, side = dis[ch], edges[16 * ch : 16 * ch + 16, :]
        at_left[ch] = jnp.where(lane < 64, side, here)
        at_right[ch] = jnp.where(lane < 64, here, side)

    def spread_row(k, i, m, c):
        at = 24 * (6 * k + 3 * i + m) + c
        return spread[at : at + 1, :]

    forces = element_sums(spread_row, (at_left, at_right), 1, scale.at[2], 0)
    lane = lanes((ROWS, COLS))
    for m in range(3):
        for k in range(2):
            ch = 2 * m + k
            change = weight[k] * jnp.where((lane == 0) | (lane == COLS - 1), forces[ch], 0.0)
            out_vel[m, k] = base_vel[ch] - change
            out_dis[m, k] = base_dis[ch] - DT * change


def call(kernel, outs, specs, scratch=(), flops=1_000_000, moved=1_000_000, room=16):
    return pl.pallas_call(
        kernel,
        out_shape=outs,
        in_specs=specs,
        out_specs=jax.tree.map(lambda _: VMEM, outs),
        scratch_shapes=list(scratch),
        compiler_params=pltpu.CompilerParams(vmem_limit_bytes=room << 20),
        cost_estimate=pl.CostEstimate(flops=flops, bytes_accessed=moved, transcendentals=0),
    )


def swapped(to_next, to_last, axis):
    size = lax.axis_size(axis)
    up = [(i, (i + 1) % size) for i in range(size)]
    down = [(j, i) for i, j in up]
    return lax.ppermute(to_next, axis, up), lax.ppermute(to_last, axis, down)


def shards(u, v, mass, mod, stiff, ref, facets, penalty, owners, pair):
    width = facets.shape[-1]
    buffers = [pltpu.VMEM((6, 24, COLS), F32)] * 3
    owner = owners.reshape(2, 1, ROWS)
    sources = (u, v, mass, mod, ref, facets.reshape(6 * width // COLS, COLS), penalty.reshape(width // COLS, COLS), pair)
    table, up, down = call(
        pack_kernel,
        (struct(OWNERS, 32, COLS), struct(MSG, COLS), struct(MSG, COLS)),
        [pl.BlockSpec(memory_space=pltpu.HBM)] * len(sources) + [SMEM],
        [pltpu.VMEM(x.shape, x.dtype) for x in sources] + [pltpu.SemaphoreType.DMA((len(sources),))],
        room=60,
    )(*sources, owner)
    tables = lax.all_to_all(table, "mesh", split_axis=0, concat_axis=0, tiled=True)
    above, below = swapped(down, up, "mesh")
    ext, left, right = call(
        extend_kernel, (struct(128, COLS), struct(1, COLS), struct(1, COLS)), [VMEM] * 4
    )(u, mod, above, below)
    from_left, from_right = swapped(right, left, "sub")
    vel, dis, weight, point, index, who, scale, spread = call(
        first_kernel,
        (
            struct(6, 16, COLS),
            struct(6, 16, COLS),
            struct(2, 16, COLS),
            struct(3, 16, COLS),
            struct(16, COLS, dtype=jnp.int32),
            struct(24, COLS, dtype=jnp.int32),
            struct(3, 24, COLS),
            struct(288, COLS),
        ),
        [SMEM] * 2 + [VMEM] * 9,
        buffers,
    )(stiff, owner, ext, from_left, from_right, above, below, v, mass, ref, pair)
    new_vel, new_dis, left, right = call(
        contact_kernel,
        (struct(6, ROWS, COLS), struct(6, 16, COLS), struct(1, COLS), struct(1, COLS)),
        [VMEM] * 7,
        [pltpu.VMEM((4, 16, COLS), F32), pltpu.VMEM((128, COLS), F32)],
    )(who, tables, index, vel, dis, weight, point)
    from_left, from_right = swapped(right, left, "sub")
    base_dis, base_vel, weight = call(
        inner_kernel,
        (struct(6, ROWS, COLS), struct(6, ROWS, COLS), struct(2, ROWS, COLS)),
        [VMEM, SMEM] + [VMEM] * 7,
        [pltpu.VMEM((6, 16, COLS), F32), pltpu.VMEM((4, 8, COLS), F32)],
    )(who, stiff, tables, pair, new_dis, new_vel, mass, ref, scale)
    return call(
        outer_kernel,
        (struct(3, 2, ROWS, COLS), struct(3, 2, ROWS, COLS)),
        [VMEM] * 8,
        [pltpu.VMEM((6, 16, COLS), F32)] * 2,
    )(new_dis, base_dis, base_vel, weight, scale, spread, from_left, from_right)


def solution(mesh):
    in_specs = (
        P(None, None, "mesh", "sub"),
        P(None, None, "mesh", "sub"),
        P(None, "mesh", "sub"),
        P(None, "mesh", "sub"),
        P(),
        P(None, "mesh", "sub"),
        P("mesh", "sub", None, None),
        P("mesh", "sub", None),
        P(None, "mesh", "sub", None, None),
        P(None, "mesh", "sub"),
    )
    out_specs = (P(None, None, "mesh", "sub"), P(None, None, "mesh", "sub"))
    return jax.shard_map(shards, mesh=mesh, in_specs=in_specs, out_specs=out_specs, check_vma=False)
```

```python
import jax
import jax.numpy as jnp
from jax import lax
from jax.experimental import pallas as pl
from jax.experimental.pallas import tpu as pltpu
from jax.sharding import PartitionSpec as P

DT = 0.1
F32 = jnp.float32
VMEM = pl.BlockSpec(memory_space=pltpu.VMEM)
HBM = pl.BlockSpec(memory_space=pltpu.HBM)
ANY = pl.BlockSpec(memory_space=pl.ANY)
SMEM = pl.BlockSpec(memory_space=pltpu.SMEM)
ROWS = 8
COLS = 128
OWNERS = 32
AT_U, AT_E, AT_V, AT_M, AT_X, AT_P, AT_O = 0, 12, 16, 22, 24, 27, 28
MSG = 32


def struct(*shape, dtype=F32):
    return jax.ShapeDtypeStruct(shape, dtype)


def lanes(shape):
    return lax.broadcasted_iota(jnp.int32, shape, len(shape) - 1)


def fetched(sources, held, sems):
    copies = [pltpu.make_async_copy(a, b, sems.at[n]) for n, (a, b) in enumerate(zip(sources, held))]
    for copy in copies:
        copy.start()
    for copy in copies:
        copy.wait()
    return held


def pack_kernel(fac, pen, u, v, mass, mod, ref, pair, own, mine, up, down, *held):
    fac, pen, u, v, mass, mod, ref, pair, own = fetched((fac, pen, u, v, mass, mod, ref, pair, own), held[:-1], held[-1])
    root = jnp.sqrt(pen[...])
    c, n = [[fac[8 * (m + at) : 8 * (m + at) + 8, :] for m in range(3)] for at in (0, 3)]
    dist = n[0] * c[0] + n[1] * c[1] + n[2] * c[2]
    words = [root * n[0], root * n[1], root * n[2], root * dist]
    for q in range(4):
        mine[8 * q : 8 * q + 8, :] = jnp.concatenate([w[4 * h + q : 4 * h + q + 1, :] for h in range(2) for w in words], axis=0)
    for out, two, one in ((down, ROWS - 2, ROWS - 1), (up, 0, 0)):
        for m in range(3):
            for k in range(2):
                ch = 2 * m + k
                out[AT_U + 2 * ch : AT_U + 2 * ch + 2, :] = u[m, k, two : two + 2, :]
                out[AT_V + ch : AT_V + ch + 1, :] = v[m, k, one : one + 1, :]
            out[AT_X + m : AT_X + m + 1, :] = ref[m, one : one + 1, :]
        for k in range(2):
            out[AT_E + 2 * k : AT_E + 2 * k + 2, :] = mod[k, two : two + 2, :]
            out[AT_M + k : AT_M + k + 1, :] = mass[k, one : one + 1, :]
        out[AT_P : AT_P + 1, :] = pair[0, one : one + 1, :].astype(F32)
        out[AT_O :, :] = jnp.zeros((MSG - AT_O, COLS), F32)
        out[AT_O : AT_O + 1, 0:ROWS] = own[0].astype(F32)


def spread_kernel(mine, above, below, table, sems):
    copies = [pltpu.make_async_copy(mine, table.at[o], sems.at[o]) for o in range(OWNERS)]
    for copy in copies:
        copy.start()
    for copy in copies:
        copy.wait()


def extend_kernel(u, mod, above, below, ext, left, right):
    for ch in range(8):
        at = AT_U + 2 * ch if ch < 6 else AT_E + 2 * (ch - 6)
        own = u[ch // 2, ch % 2] if ch < 6 else mod[ch - 6]
        ext[16 * ch : 16 * ch + 2, :] = above[at : at + 2, :]
        ext[16 * ch + 2 : 16 * ch + 10, :] = own
        ext[16 * ch + 10 : 16 * ch + 12, :] = below[at : at + 2, :]
        ext[16 * ch + 12 : 16 * ch + 16, :] = jnp.zeros((4, COLS), F32)
    turned = jnp.transpose(ext[...])
    left[...] = turned[0:1, :]
    right[...] = turned[COLS - 1 : COLS, :]


def edge_columns(from_left, from_right):
    sub = lax.broadcasted_iota(jnp.int32, (128, COLS), 0)
    both = jnp.where(sub < 64, jnp.broadcast_to(from_left, (128, COLS)), jnp.broadcast_to(from_right, (128, COLS)))
    return jnp.transpose(both)


def with_columns(here, edges):
    lane = lanes(here.shape)
    return jnp.where(lane == COLS - 1, edges, pltpu.roll(here, COLS - 1, axis=1))


def corners():
    return [(3 * (4 * k + 2 * x + e) + m, 2 * m + k, x, e) for k in range(2) for x in range(2) for e in range(2) for m in range(3)]


def element_sums(weight, rows_of, sides, scales, at):
    total = {}
    for i in range(2):
        start = at + 1 - i
        values = {c: rows_of[e][ch, pl.ds(start + x, ROWS), :] for c, ch, x, e in corners()}
        for k in range(2):
            for m in range(3):
                force = None
                for c in range(24):
                    t = weight(k, i, m, c) * values[c]
                    force = t if force is None else force + t
                force = force * scales[pl.ds(start + sides, ROWS), :]
                total[2 * m + k] = force if i == 0 else total[2 * m + k] + force
    return [total[ch] for ch in range(6)]


def by_corner(stiff, e):
    return lambda k, i, m, c: stiff[3 * (4 * k + 2 * i + e) + m, c]


def first_kernel(stiff, owner, ext, from_left, from_right, above, below, v, mass, ref, pair, vel, dis, weight, point, index, who, scale, spread, at_left, at_right, at_edge):
    edges = edge_columns(from_left[...], from_right[...])
    zero = jnp.zeros((8, COLS), F32)
    lane = lanes((ROWS, COLS))
    for ch in range(6):
        here, side = ext[16 * ch : 16 * ch + 16, :], edges[16 * ch : 16 * ch + 16, :]
        at_left[ch, 0:16, :] = here
        at_right[ch, 0:16, :] = with_columns(here, side)
        at_edge[ch, 0:16, :] = side
        for buf in (at_left, at_right, at_edge):
            buf[ch, 16:24, :] = zero
    here = ext[96:112, :] + ext[112:128, :]
    side = edges[96:112, :] + edges[112:128, :]
    right = with_columns(here, side)
    for n, both in enumerate((here + right, side + here)):
        scale[n, 0:16, :] = (both + pltpu.roll(both, 15, axis=0)) * 0.125
        scale[n, 16:24, :] = zero
    for k in range(2):
        weight[k, 0:1, :] = above[AT_M + k : AT_M + k + 1, :]
        weight[k, 1:9, :] = mass[k]
        weight[k, 9:10, :] = below[AT_M + k : AT_M + k + 1, :]
        weight[k, 10:16, :] = jnp.ones((6, COLS), F32)
        weight[k] = DT / weight[k]
    for ch in range(6):
        vel[ch, 0:1, :] = above[AT_V + ch : AT_V + ch + 1, :]
        vel[ch, 1:9, :] = v[ch // 2, ch % 2]
        vel[ch, 9:10, :] = below[AT_V + ch : AT_V + ch + 1, :]
        vel[ch, 10:16, :] = zero[:6]
    for m in range(3):
        point[m, 0:1, :] = above[AT_X + m : AT_X + m + 1, :]
        point[m, 1:9, :] = ref[m]
        point[m, 9:10, :] = below[AT_X + m : AT_X + m + 1, :]
        point[m, 10:16, :] = zero[:6]
        point[m] = point[m] + at_left[2 * m, 1:17, :]
    index[0:1, :] = above[AT_P : AT_P + 1, :].astype(jnp.int32)
    index[1:9, :] = pair[0]
    index[9:10, :] = below[AT_P : AT_P + 1, :].astype(jnp.int32)
    index[10:16, :] = jnp.zeros((6, COLS), jnp.int32)
    who[...] = jnp.zeros((8, COLS), jnp.int32)
    who[0:1, :] = above[AT_O : AT_O + 1, :].astype(jnp.int32)
    who[1:2, :] = below[AT_O : AT_O + 1, :].astype(jnp.int32)
    for step in range(2):
        who[2 + step : 3 + step, 0:ROWS] = owner[step]
    for at in (0, 8):
        straight = element_sums(by_corner(stiff, 0), (at_left, at_right), 0, scale.at[0], at)
        moved = element_sums(by_corner(stiff, 1), (at_left, at_right), 0, scale.at[0], at)
        edge = element_sums(by_corner(stiff, 1), (at_edge, at_left), 0, scale.at[1], at)
        for ch in range(6):
            force = straight[ch] + jnp.where(lane == 0, edge[ch], pltpu.roll(moved[ch], 1, axis=1))
            new = vel[ch, at : at + 8, :] - weight[ch % 2, at : at + 8, :] * force
            vel[ch, at : at + 8, :] = new
            dis[ch, at : at + 8, :] = at_left[ch, at + 1 : at + 9, :] + DT * new
    row = lanes((1, COLS))
    for k in range(2):
        for i in range(2):
            for m in range(3):
                for c in range(24):
                    one, other = [stiff[3 * (4 * k + 2 * i + e) + m, c] for e in (1, 0)]
                    at = 24 * (6 * k + 3 * i + m) + c
                    spread[at : at + 1, :] = jnp.where(row < 64, one, other)
    scale[2] = jnp.where(lanes((24, COLS)) < 64, scale[1], scale[0])


def look_up(table, owner, index, row, out):
    which = jnp.broadcast_to(index, (8, COLS))
    place, part = which & 127, (which >> 7) & 3
    found = None
    for c in range(4):
        got = jnp.take_along_axis(table[owner, 8 * c : 8 * c + 8, :], place, axis=1)
        found = got if found is None else jnp.where(part == c, got, found)
    found = jnp.where(which[0:4] >= 512, found[4:8], found[0:4])
    for c in range(4):
        out[c, row : row + 1, :] = found[c : c + 1]


def contact(words, points):
    depth = jnp.maximum(words[3] - (words[0] * points[0] + words[1] * points[1] + words[2] * points[2]), 0.0)
    return [words[m] * depth for m in range(3)]


def contact_kernel(who, table, index, vel, dis, weight, point, new_vel, new_dis, left, right, words, square):
    words[:, 8:16, :] = jnp.zeros((4, 8, COLS), F32)
    for b in range(ROWS + 2):
        look_up(table, who[0, ROWS - 1] if b == 0 else who[1, 0] if b == ROWS + 1 else who[2, b - 1], index[b : b + 1, :], b, words)
    pushes = contact([words[c] for c in range(4)], [point[m] for m in range(3)])
    for m in range(3):
        step = weight[0] * pushes[m]
        new_vel[2 * m] = (vel[2 * m] + step)[1:9]
        new_vel[2 * m + 1] = vel[2 * m + 1, 1:9, :]
        new_dis[2 * m] = dis[2 * m] + DT * step
        new_dis[2 * m + 1] = dis[2 * m + 1]
    for ch in range(6):
        square[16 * ch : 16 * ch + 16, :] = new_dis[ch]
    square[96:128, :] = jnp.zeros((32, COLS), F32)
    turned = jnp.transpose(square[...])
    left[...] = turned[0:1, :]
    right[...] = turned[COLS - 1 : COLS, :]


def inner_kernel(who, stiff, table, pair, dis, vel, mass, ref, scale, base_dis, base_vel, weight, at_right, words):
    lane = lanes((ROWS, COLS))
    for b in range(ROWS):
        look_up(table, who[3, b], pair[1, b : b + 1, :], b, words)
    push = contact([words[c] for c in range(4)], [ref[m] + dis[2 * m, 1:9, :] for m in range(3)])
    for ch in range(6):
        at_right[ch] = pltpu.roll(dis[ch], COLS - 1, axis=1)
    straight = element_sums(by_corner(stiff, 0), (dis, at_right), 1, scale.at[0], 0)
    moved = element_sums(by_corner(stiff, 1), (dis, at_right), 1, scale.at[0], 0)
    for k in range(2):
        weight[k] = DT / mass[k]
        for m in range(3):
            ch = 2 * m + k
            force = jnp.where(lane == COLS - 1, 0.0, straight[ch]) + jnp.where(lane == 0, 0.0, pltpu.roll(moved[ch], 1, axis=1))
            net = push[m] - force if k == 0 else -force
            new = vel[ch] + weight[k] * net
            base_vel[ch] = new
            base_dis[ch] = dis[ch, 1:9, :] + DT * new


def outer_kernel(dis, base_dis, base_vel, weight, scale, spread, from_left, from_right, out_dis, out_vel, at_left, at_right):
    edges = edge_columns(from_left[...], from_right[...])
    lane = lanes((16, COLS))
    for ch in range(6):
        here, side = dis[ch], edges[16 * ch : 16 * ch + 16, :]
        at_left[ch] = jnp.where(lane < 64, side, here)
        at_right[ch] = jnp.where(lane < 64, here, side)

    def spread_row(k, i, m, c):
        at = 24 * (6 * k + 3 * i + m) + c
        return spread[at : at + 1, :]

    forces = element_sums(spread_row, (at_left, at_right), 1, scale.at[2], 0)
    lane = lanes((ROWS, COLS))
    for m in range(3):
        for k in range(2):
            ch = 2 * m + k
            change = weight[k] * jnp.where((lane == 0) | (lane == COLS - 1), forces[ch], 0.0)
            out_vel[m, k] = base_vel[ch] - change
            out_dis[m, k] = base_dis[ch] - DT * change


def call(kernel, outs, specs, scratch=(), room=16, out_specs=None, flops=1_000_000, moved=1_000_000):
    return pl.pallas_call(
        kernel,
        out_shape=outs,
        in_specs=specs,
        out_specs=out_specs or jax.tree.map(lambda _: VMEM, outs),
        scratch_shapes=list(scratch),
        compiler_params=pltpu.CompilerParams(vmem_limit_bytes=room << 20),
        cost_estimate=pl.CostEstimate(flops=flops, bytes_accessed=moved, transcendentals=0),
    )


def swapped(to_next, to_last, axis):
    size = lax.axis_size(axis)
    up = [(i, (i + 1) % size) for i in range(size)]
    down = [(j, i) for i, j in up]
    return lax.ppermute(to_next, axis, up), lax.ppermute(to_last, axis, down)


def shards(u, v, mass, mod, stiff, ref, facets, penalty, owners, pair):
    width = facets.shape[-1]
    buffers = [pltpu.VMEM((6, 24, COLS), F32)] * 3
    owner = owners.reshape(2, 1, ROWS)
    sources = (
        facets.reshape(6 * width // COLS, COLS),
        penalty.reshape(width // COLS, COLS),
        *(u, v, mass, mod, ref, pair, owner),
    )
    mine, up, down = call(
        pack_kernel,
        (struct(32, COLS), struct(MSG, COLS), struct(MSG, COLS)),
        [HBM] * len(sources),
        [pltpu.VMEM(x.shape, x.dtype) for x in sources] + [pltpu.SemaphoreType.DMA((len(sources),))],
        room=60,
    )(*sources)
    above, below = swapped(down, up, "mesh")
    table = call(
        spread_kernel,
        struct(OWNERS, 32, COLS),
        [HBM, ANY, ANY],
        [pltpu.SemaphoreType.DMA((OWNERS,))],
        out_specs=HBM,
        flops=0,
        moved=0,
    )(mine, above, below)
    tables = lax.all_to_all(table, "mesh", split_axis=0, concat_axis=0, tiled=True)
    ext, left, right = call(
        extend_kernel, (struct(128, COLS), struct(1, COLS), struct(1, COLS)), [VMEM] * 4
    )(u, mod, above, below)
    from_left, from_right = swapped(right, left, "sub")
    vel, dis, weight, point, index, who, scale, spread = call(
        first_kernel,
        (
            struct(6, 16, COLS),
            struct(6, 16, COLS),
            struct(2, 16, COLS),
            struct(3, 16, COLS),
            struct(16, COLS, dtype=jnp.int32),
            struct(8, COLS, dtype=jnp.int32),
            struct(3, 24, COLS),
            struct(288, COLS),
        ),
        [SMEM] + [VMEM] * 10,
        buffers,
    )(stiff, owner, ext, from_left, from_right, above, below, v, mass, ref, pair)
    new_vel, new_dis, left, right = call(
        contact_kernel,
        (struct(6, ROWS, COLS), struct(6, 16, COLS), struct(1, COLS), struct(1, COLS)),
        [VMEM] * 7,
        [pltpu.VMEM((4, 16, COLS), F32), pltpu.VMEM((128, COLS), F32)],
    )(who, tables, index, vel, dis, weight, point)
    from_left, from_right = swapped(right, left, "sub")
    base_dis, base_vel, weight = call(
        inner_kernel,
        (struct(6, ROWS, COLS), struct(6, ROWS, COLS), struct(2, ROWS, COLS)),
        [VMEM, SMEM] + [VMEM] * 7,
        [pltpu.VMEM((6, 16, COLS), F32), pltpu.VMEM((4, 8, COLS), F32)],
    )(who, stiff, tables, pair, new_dis, new_vel, mass, ref, scale)
    return call(
        outer_kernel,
        (struct(3, 2, ROWS, COLS), struct(3, 2, ROWS, COLS)),
        [VMEM] * 8,
        [pltpu.VMEM((6, 16, COLS), F32)] * 2,
    )(new_dis, base_dis, base_vel, weight, scale, spread, from_left, from_right)


def solution(mesh):
    in_specs = (
        P(None, None, "mesh", "sub"),
        P(None, None, "mesh", "sub"),
        P(None, "mesh", "sub"),
        P(None, "mesh", "sub"),
        P(),
        P(None, "mesh", "sub"),
        P("mesh", "sub", None, None),
        P("mesh", "sub", None),
        P(None, "mesh", "sub", None, None),
        P(None, "mesh", "sub"),
    )
    out_specs = (P(None, None, "mesh", "sub"), P(None, None, "mesh", "sub"))
    return jax.shard_map(shards, mesh=mesh, in_specs=in_specs, out_specs=out_specs, check_vma=False)
```

```python
import jax
import jax.numpy as jnp
from jax import lax
from jax.experimental import pallas as pl
from jax.experimental.pallas import tpu as pltpu
from jax.sharding import PartitionSpec as P

DT = 0.1
F32 = jnp.float32
VMEM = pl.BlockSpec(memory_space=pltpu.VMEM)
HBM = pl.BlockSpec(memory_space=pltpu.HBM)
SMEM = pl.BlockSpec(memory_space=pltpu.SMEM)
ROWS = 8
COLS = 128
OWNERS = 32
AT_U, AT_E, AT_V, AT_M, AT_X, AT_P, AT_O, AT_L, AT_R = 0, 12, 16, 22, 24, 27, 28, 29, 30
MSG = 32


def struct(*shape, dtype=F32):
    return jax.ShapeDtypeStruct(shape, dtype)


def lanes(shape):
    return lax.broadcasted_iota(jnp.int32, shape, len(shape) - 1)


def table_kernel(fac, pen, u, mod, table, left, right, fac_, pen_, u_, mod_, mine, square, sems, out_sems):
    copies = [pltpu.make_async_copy(a, b, sems.at[n]) for n, (a, b) in enumerate(zip((fac, pen, u, mod), (fac_, pen_, u_, mod_)))]
    for copy in copies:
        copy.start()
    for copy in copies:
        copy.wait()
    root = jnp.sqrt(pen_[...])
    c, n = [[fac_[8 * (m + at) : 8 * (m + at) + 8, :] for m in range(3)] for at in (0, 3)]
    dist = n[0] * c[0] + n[1] * c[1] + n[2] * c[2]
    words = [root * n[0], root * n[1], root * n[2], root * dist]
    for q in range(4):
        mine[8 * q : 8 * q + 8, :] = jnp.concatenate([w[4 * h + q : 4 * h + q + 1, :] for h in range(2) for w in words], axis=0)
    outs = [pltpu.make_async_copy(mine, table.at[o], out_sems.at[o]) for o in range(OWNERS)]
    for copy in outs:
        copy.start()
    for ch in range(8):
        square[16 * ch : 16 * ch + 8, :] = u_[ch // 2, ch % 2] if ch < 6 else mod_[ch - 6]
        square[16 * ch + 8 : 16 * ch + 16, :] = jnp.zeros((8, COLS), F32)
    turned = jnp.transpose(square[...])
    left[...] = turned[0:1, :]
    right[...] = turned[COLS - 1 : COLS, :]
    for copy in outs:
        copy.wait()


def pack_kernel(u, v, mass, mod, ref, pair, own, from_left, from_right, up, down):
    for out, two, one in ((down, ROWS - 2, ROWS - 1), (up, 0, 0)):
        for m in range(3):
            for k in range(2):
                ch = 2 * m + k
                out[AT_U + 2 * ch : AT_U + 2 * ch + 2, :] = u[m, k, two : two + 2, :]
                out[AT_V + ch : AT_V + ch + 1, :] = v[m, k, one : one + 1, :]
            out[AT_X + m : AT_X + m + 1, :] = ref[m, one : one + 1, :]
        for k in range(2):
            out[AT_E + 2 * k : AT_E + 2 * k + 2, :] = mod[k, two : two + 2, :]
            out[AT_M + k : AT_M + k + 1, :] = mass[k, one : one + 1, :]
        out[AT_P : AT_P + 1, :] = pair[0, one : one + 1, :].astype(F32)
        out[AT_O :, :] = jnp.zeros((MSG - AT_O, COLS), F32)
        out[AT_O : AT_O + 1, 0:ROWS] = own[0].astype(F32)
        out[AT_L : AT_L + 1, :] = from_left[...]
        out[AT_R : AT_R + 1, :] = from_right[...]


def extended(here, above, below):
    here, above, below = [jnp.broadcast_to(x, (8, COLS)) for x in (here, above, below)]
    at = lanes((8, COLS)) & 15
    out = jnp.where(at < 12, pltpu.roll(below, 10, axis=1), 0.0)
    out = jnp.where(at < 10, pltpu.roll(here, 2, axis=1), out)
    return jnp.where(at < 2, pltpu.roll(above, COLS - 6, axis=1), out)[0:1]


def edge_columns(from_left, from_right):
    sub = lax.broadcasted_iota(jnp.int32, (128, COLS), 0)
    both = jnp.where(sub < 64, jnp.broadcast_to(from_left, (128, COLS)), jnp.broadcast_to(from_right, (128, COLS)))
    return jnp.transpose(both)


def with_columns(here, edges):
    lane = lanes(here.shape)
    return jnp.where(lane == COLS - 1, edges, pltpu.roll(here, COLS - 1, axis=1))


def corners():
    return [(3 * (4 * k + 2 * x + e) + m, 2 * m + k, x, e) for k in range(2) for x in range(2) for e in range(2) for m in range(3)]


def element_sums(weight, rows_of, sides, scales, at):
    total = {}
    for i in range(2):
        start = at + 1 - i
        values = {c: rows_of[e][ch, pl.ds(start + x, ROWS), :] for c, ch, x, e in corners()}
        for k in range(2):
            for m in range(3):
                force = None
                for c in range(24):
                    t = weight(k, i, m, c) * values[c]
                    force = t if force is None else force + t
                force = force * scales[pl.ds(start + sides, ROWS), :]
                total[2 * m + k] = force if i == 0 else total[2 * m + k] + force
    return [total[ch] for ch in range(6)]


def by_corner(stiff, e):
    return lambda k, i, m, c: stiff[3 * (4 * k + 2 * i + e) + m, c]


def first_kernel(stiff, owner, spread, from_left, from_right, above, below, u, v, mass, mod, ref, pair, vel, dis, weight, point, index, who, scale, at_left, at_right, at_edge):
    edges = edge_columns(
        extended(from_left[...], above[AT_L : AT_L + 1, :], below[AT_L : AT_L + 1, :]),
        extended(from_right[...], above[AT_R : AT_R + 1, :], below[AT_R : AT_R + 1, :]),
    )
    zero = jnp.zeros((8, COLS), F32)
    lane = lanes((16, COLS))
    for ch in range(8):
        at = AT_U + 2 * ch if ch < 6 else AT_E + 2 * (ch - 6)
        at_left[ch, 0:2, :] = above[at : at + 2, :]
        at_left[ch, 2:10, :] = u[ch // 2, ch % 2] if ch < 6 else mod[ch - 6]
        at_left[ch, 10:12, :] = below[at : at + 2, :]
        at_left[ch, 12:16, :] = zero[:4]
        side = edges[16 * ch : 16 * ch + 16, :]
        at_right[ch, 0:16, :] = with_columns(at_left[ch, 0:16, :], side)
        at_edge[ch, 0:16, :] = side
        for buf in (at_left, at_right, at_edge):
            buf[ch, 16:24, :] = zero
    here, right, side = [buf[6, 0:16, :] + buf[7, 0:16, :] for buf in (at_left, at_right, at_edge)]
    for n, both in enumerate((here + right, side + here)):
        scale[n, 0:16, :] = (both + pltpu.roll(both, 15, axis=0)) * 0.125
        scale[n, 16:24, :] = zero
    scale[2] = jnp.where(lanes((24, COLS)) < 64, scale[1], scale[0])
    for k in range(2):
        weight[k, 0:1, :] = above[AT_M + k : AT_M + k + 1, :]
        weight[k, 1:9, :] = mass[k]
        weight[k, 9:10, :] = below[AT_M + k : AT_M + k + 1, :]
        weight[k, 10:16, :] = jnp.ones((6, COLS), F32)
        weight[k] = DT / weight[k]
    for ch in range(6):
        vel[ch, 0:1, :] = above[AT_V + ch : AT_V + ch + 1, :]
        vel[ch, 1:9, :] = v[ch // 2, ch % 2]
        vel[ch, 9:10, :] = below[AT_V + ch : AT_V + ch + 1, :]
        vel[ch, 10:16, :] = zero[:6]
    for m in range(3):
        point[m, 0:1, :] = above[AT_X + m : AT_X + m + 1, :]
        point[m, 1:9, :] = ref[m]
        point[m, 9:10, :] = below[AT_X + m : AT_X + m + 1, :]
        point[m, 10:16, :] = zero[:6]
        point[m] = point[m] + at_left[2 * m, 1:17, :]
    index[0:1, :] = above[AT_P : AT_P + 1, :].astype(jnp.int32)
    index[1:9, :] = pair[0]
    index[9:10, :] = below[AT_P : AT_P + 1, :].astype(jnp.int32)
    index[10:16, :] = jnp.zeros((6, COLS), jnp.int32)
    who[...] = jnp.zeros((8, COLS), jnp.int32)
    who[0:1, :] = above[AT_O : AT_O + 1, :].astype(jnp.int32)
    who[1:2, :] = below[AT_O : AT_O + 1, :].astype(jnp.int32)
    for step in range(2):
        who[2 + step : 3 + step, 0:ROWS] = owner[step]
    del spread
    straight, moved, edge = {}, {}, {}
    for i in range(2):
        start = 1 - i
        s_main, s_edge = [scale[n, start : start + 16, :] for n in range(2)]
        for k in range(2):
            for m in range(3):
                sums = [None, None, None]
                for c, ch, x, e in corners():
                    rows = slice(start + x, start + x + 16)
                    near = at_left[ch, rows, :]
                    main, side = (at_right[ch, rows, :], near) if e else (near, at_edge[ch, rows, :])
                    w0, w1 = [stiff[3 * (4 * k + 2 * i + end) + m, c] for end in range(2)]
                    terms = (w0 * main, w1 * main, w1 * side)
                    sums = [t if s is None else s + t for s, t in zip(sums, terms)]
                for into, s, by in zip((straight, moved, edge), sums, (s_main, s_main, s_edge)):
                    into[2 * m + k] = s * by if i == 0 else into[2 * m + k] + s * by
    for ch in range(6):
        force = straight[ch] + jnp.where(lane == 0, edge[ch], pltpu.roll(moved[ch], 1, axis=1))
        new = vel[ch] - weight[ch % 2] * force
        vel[ch] = new
        dis[ch] = at_left[ch, 1:17, :] + DT * new


def spread_kernel(stiff, spread):
    lane = lanes((1, COLS))
    for k in range(2):
        for i in range(2):
            for m in range(3):
                for c in range(24):
                    one, other = [stiff[3 * (4 * k + 2 * i + e) + m, c] for e in (1, 0)]
                    at = 24 * (6 * k + 3 * i + m) + c
                    spread[at : at + 1, :] = jnp.where(lane < 64, one, other)


def look_up(table, owner, index, row, out):
    which = jnp.broadcast_to(index, (8, COLS))
    place, part = which & 127, (which >> 7) & 3
    found = None
    for c in range(4):
        got = jnp.take_along_axis(table[owner, 8 * c : 8 * c + 8, :], place, axis=1)
        found = got if found is None else jnp.where(part == c, got, found)
    found = jnp.where(which[0:4] >= 512, found[4:8], found[0:4])
    for c in range(4):
        out[c, row : row + 1, :] = found[c : c + 1]


def contact(words, points):
    depth = jnp.maximum(words[3] - (words[0] * points[0] + words[1] * points[1] + words[2] * points[2]), 0.0)
    return [words[m] * depth for m in range(3)]


def contact_kernel(who, table, index, vel, dis, weight, point, new_vel, new_dis, left, right, words, square):
    words[:, 8:16, :] = jnp.zeros((4, 8, COLS), F32)
    for b in range(ROWS + 2):
        look_up(table, who[0, ROWS - 1] if b == 0 else who[1, 0] if b == ROWS + 1 else who[2, b - 1], index[b : b + 1, :], b, words)
    pushes = contact([words[c] for c in range(4)], [point[m] for m in range(3)])
    for m in range(3):
        step = weight[0] * pushes[m]
        new_vel[2 * m] = (vel[2 * m] + step)[1:9]
        new_vel[2 * m + 1] = vel[2 * m + 1, 1:9, :]
        new_dis[2 * m] = dis[2 * m] + DT * step
        new_dis[2 * m + 1] = dis[2 * m + 1]
    for ch in range(6):
        square[16 * ch : 16 * ch + 16, :] = new_dis[ch]
    square[96:128, :] = jnp.zeros((32, COLS), F32)
    turned = jnp.transpose(square[...])
    left[...] = turned[0:1, :]
    right[...] = turned[COLS - 1 : COLS, :]


def inner_kernel(who, stiff, table, pair, dis, vel, mass, ref, scale, base_dis, base_vel, weight, at_right, words):
    lane = lanes((ROWS, COLS))
    for b in range(ROWS):
        look_up(table, who[3, b], pair[1, b : b + 1, :], b, words)
    push = contact([words[c] for c in range(4)], [ref[m] + dis[2 * m, 1:9, :] for m in range(3)])
    for ch in range(6):
        at_right[ch] = pltpu.roll(dis[ch], COLS - 1, axis=1)
    straight = element_sums(by_corner(stiff, 0), (dis, at_right), 1, scale.at[0], 0)
    moved = element_sums(by_corner(stiff, 1), (dis, at_right), 1, scale.at[0], 0)
    for k in range(2):
        weight[k] = DT / mass[k]
        for m in range(3):
            ch = 2 * m + k
            force = jnp.where(lane == COLS - 1, 0.0, straight[ch]) + jnp.where(lane == 0, 0.0, pltpu.roll(moved[ch], 1, axis=1))
            net = push[m] - force if k == 0 else -force
            new = vel[ch] + weight[k] * net
            base_vel[ch] = new
            base_dis[ch] = dis[ch, 1:9, :] + DT * new


def outer_kernel(dis, base_dis, base_vel, weight, scale, spread, from_left, from_right, out_dis, out_vel, at_left, at_right):
    edges = edge_columns(from_left[...], from_right[...])
    lane = lanes((16, COLS))
    for ch in range(6):
        here, side = dis[ch], edges[16 * ch : 16 * ch + 16, :]
        at_left[ch] = jnp.where(lane < 64, side, here)
        at_right[ch] = jnp.where(lane < 64, here, side)

    def spread_row(k, i, m, c):
        at = 24 * (6 * k + 3 * i + m) + c
        return spread[at : at + 1, :]

    forces = element_sums(spread_row, (at_left, at_right), 1, scale.at[2], 0)
    lane = lanes((ROWS, COLS))
    for m in range(3):
        for k in range(2):
            ch = 2 * m + k
            change = weight[k] * jnp.where((lane == 0) | (lane == COLS - 1), forces[ch], 0.0)
            out_vel[m, k] = base_vel[ch] - change
            out_dis[m, k] = base_dis[ch] - DT * change


def call(kernel, outs, specs, scratch=(), room=16, out_specs=None, flops=1_000_000, moved=1_000_000):
    return pl.pallas_call(
        kernel,
        out_shape=outs,
        in_specs=specs,
        out_specs=out_specs or jax.tree.map(lambda _: VMEM, outs),
        scratch_shapes=list(scratch),
        compiler_params=pltpu.CompilerParams(vmem_limit_bytes=room << 20),
        cost_estimate=pl.CostEstimate(flops=flops, bytes_accessed=moved, transcendentals=0),
    )


def swapped(to_next, to_last, axis):
    size = lax.axis_size(axis)
    up = [(i, (i + 1) % size) for i in range(size)]
    down = [(j, i) for i, j in up]
    return lax.ppermute(to_next, axis, up), lax.ppermute(to_last, axis, down)


def shards(u, v, mass, mod, stiff, ref, facets, penalty, owners, pair):
    width = facets.shape[-1]
    owner = owners.reshape(2, 1, ROWS)
    sources = (facets.reshape(6 * width // COLS, COLS), penalty.reshape(width // COLS, COLS), u, mod)
    table, left, right = call(
        table_kernel,
        (struct(OWNERS, 32, COLS), struct(1, COLS), struct(1, COLS)),
        [HBM] * 4,
        [pltpu.VMEM(x.shape, x.dtype) for x in sources]
        + [pltpu.VMEM((32, COLS), F32), pltpu.VMEM((128, COLS), F32)]
        + [pltpu.SemaphoreType.DMA((n,)) for n in (4, OWNERS)],
        room=60,
        out_specs=(HBM, VMEM, VMEM),
    )(*sources)
    tables = lax.all_to_all(table, "mesh", split_axis=0, concat_axis=0, tiled=True)
    from_left, from_right = swapped(right, left, "sub")
    up, down = call(pack_kernel, (struct(MSG, COLS), struct(MSG, COLS)), [VMEM] * 9)(
        u, v, mass, mod, ref, pair, owner, from_left, from_right
    )
    above, below = swapped(down, up, "mesh")
    spread = call(spread_kernel, struct(288, COLS), [SMEM])(stiff)
    vel, dis, weight, point, index, who, scale = call(
        first_kernel,
        (
            struct(6, 16, COLS),
            struct(6, 16, COLS),
            struct(2, 16, COLS),
            struct(3, 16, COLS),
            struct(16, COLS, dtype=jnp.int32),
            struct(8, COLS, dtype=jnp.int32),
            struct(3, 24, COLS),
        ),
        [SMEM] + [VMEM] * 12,
        [pltpu.VMEM((8, 24, COLS), F32)] * 3,
    )(stiff, owner, spread, from_left, from_right, above, below, u, v, mass, mod, ref, pair)
    new_vel, new_dis, left, right = call(
        contact_kernel,
        (struct(6, ROWS, COLS), struct(6, 16, COLS), struct(1, COLS), struct(1, COLS)),
        [VMEM] * 7,
        [pltpu.VMEM((4, 16, COLS), F32), pltpu.VMEM((128, COLS), F32)],
    )(who, tables, index, vel, dis, weight, point)
    from_left, from_right = swapped(right, left, "sub")
    base_dis, base_vel, weight = call(
        inner_kernel,
        (struct(6, ROWS, COLS), struct(6, ROWS, COLS), struct(2, ROWS, COLS)),
        [VMEM, SMEM] + [VMEM] * 7,
        [pltpu.VMEM((6, 16, COLS), F32), pltpu.VMEM((4, 8, COLS), F32)],
    )(who, stiff, tables, pair, new_dis, new_vel, mass, ref, scale)
    return call(
        outer_kernel,
        (struct(3, 2, ROWS, COLS), struct(3, 2, ROWS, COLS)),
        [VMEM] * 8,
        [pltpu.VMEM((6, 16, COLS), F32)] * 2,
    )(new_dis, base_dis, base_vel, weight, scale, spread, from_left, from_right)


def solution(mesh):
    in_specs = (
        P(None, None, "mesh", "sub"),
        P(None, None, "mesh", "sub"),
        P(None, "mesh", "sub"),
        P(None, "mesh", "sub"),
        P(),
        P(None, "mesh", "sub"),
        P("mesh", "sub", None, None),
        P("mesh", "sub", None),
        P(None, "mesh", "sub", None, None),
        P(None, "mesh", "sub"),
    )
    out_specs = (P(None, None, "mesh", "sub"), P(None, None, "mesh", "sub"))
    return jax.shard_map(shards, mesh=mesh, in_specs=in_specs, out_specs=out_specs, check_vma=False)
```

```python
import jax
import jax.numpy as jnp
from jax import lax
from jax.experimental import pallas as pl
from jax.experimental.pallas import tpu as pltpu
from jax.sharding import PartitionSpec as P

DT = 0.1
F32 = jnp.float32
VMEM = pl.BlockSpec(memory_space=pltpu.VMEM)
HBM = pl.BlockSpec(memory_space=pltpu.HBM)
SMEM = pl.BlockSpec(memory_space=pltpu.SMEM)
ROWS = 8
COLS = 128
OWNERS = 32
REPLICAS = 8
AT_U, AT_E, AT_V, AT_M, AT_X, AT_P, AT_O, AT_L, AT_R = 0, 12, 16, 22, 24, 27, 28, 29, 30
MSG = 32


def struct(*shape, dtype=F32):
    return jax.ShapeDtypeStruct(shape, dtype)


def lanes(shape):
    return lax.broadcasted_iota(jnp.int32, shape, len(shape) - 1)


def table_kernel(fac, pen, table, fac_, pen_, mine, sems, out_sems):
    copies = [pltpu.make_async_copy(a, b, sems.at[n]) for n, (a, b) in enumerate(((fac, fac_), (pen, pen_)))]
    for copy in copies:
        copy.start()
    for copy in copies:
        copy.wait()
    root = jnp.sqrt(pen_[...])
    c, n = [[fac_[8 * (m + at) : 8 * (m + at) + 8, :] for m in range(3)] for at in (0, 3)]
    dist = n[0] * c[0] + n[1] * c[1] + n[2] * c[2]
    words = [root * n[0], root * n[1], root * n[2], root * dist]
    for q in range(4):
        tile = jnp.concatenate([w[4 * h + q : 4 * h + q + 1, :] for h in range(2) for w in words], axis=0)
        for r in range(REPLICAS):
            mine[r, 8 * q : 8 * q + 8, :] = tile
    outs = [pltpu.make_async_copy(mine, table.at[pl.ds(o * REPLICAS, REPLICAS)], out_sems.at[o]) for o in range(OWNERS // REPLICAS)]
    for copy in outs:
        copy.start()
    for copy in outs:
        copy.wait()


def columns_kernel(u, mod, left, right, square):
    for ch in range(8):
        square[16 * ch : 16 * ch + 8, :] = u[ch // 2, ch % 2] if ch < 6 else mod[ch - 6]
        square[16 * ch + 8 : 16 * ch + 16, :] = jnp.zeros((8, COLS), F32)
    turned = jnp.transpose(square[...])
    left[...] = turned[0:1, :]
    right[...] = turned[COLS - 1 : COLS, :]


def pack_kernel(u, v, mass, mod, ref, pair, own, from_left, from_right, up, down):
    for out, two, one in ((down, ROWS - 2, ROWS - 1), (up, 0, 0)):
        for m in range(3):
            for k in range(2):
                ch = 2 * m + k
                out[AT_U + 2 * ch : AT_U + 2 * ch + 2, :] = u[m, k, two : two + 2, :]
                out[AT_V + ch : AT_V + ch + 1, :] = v[m, k, one : one + 1, :]
            out[AT_X + m : AT_X + m + 1, :] = ref[m, one : one + 1, :]
        for k in range(2):
            out[AT_E + 2 * k : AT_E + 2 * k + 2, :] = mod[k, two : two + 2, :]
            out[AT_M + k : AT_M + k + 1, :] = mass[k, one : one + 1, :]
        out[AT_P : AT_P + 1, :] = pair[0, one : one + 1, :].astype(F32)
        out[AT_O :, :] = jnp.zeros((MSG - AT_O, COLS), F32)
        out[AT_O : AT_O + 1, 0:ROWS] = own[0].astype(F32)
        out[AT_L : AT_L + 1, :] = from_left[...]
        out[AT_R : AT_R + 1, :] = from_right[...]


def extended(here, above, below):
    here, above, below = [jnp.broadcast_to(x, (8, COLS)) for x in (here, above, below)]
    at = lanes((8, COLS)) & 15
    out = jnp.where(at < 12, pltpu.roll(below, 10, axis=1), 0.0)
    out = jnp.where(at < 10, pltpu.roll(here, 2, axis=1), out)
    return jnp.where(at < 2, pltpu.roll(above, COLS - 6, axis=1), out)[0:1]


def edge_columns(from_left, from_right):
    sub = lax.broadcasted_iota(jnp.int32, (128, COLS), 0)
    both = jnp.where(sub < 64, jnp.broadcast_to(from_left, (128, COLS)), jnp.broadcast_to(from_right, (128, COLS)))
    return jnp.transpose(both)


def with_columns(here, edges):
    lane = lanes(here.shape)
    return jnp.where(lane == COLS - 1, edges, pltpu.roll(here, COLS - 1, axis=1))


def corners():
    return [(3 * (4 * k + 2 * x + e) + m, 2 * m + k, x, e) for k in range(2) for x in range(2) for e in range(2) for m in range(3)]


def element_sums(weight, rows_of, sides, scales, at):
    total = {}
    for i in range(2):
        start = at + 1 - i
        values = {c: rows_of[e][ch, pl.ds(start + x, ROWS), :] for c, ch, x, e in corners()}
        for k in range(2):
            for m in range(3):
                force = None
                for c in range(24):
                    t = weight(k, i, m, c) * values[c]
                    force = t if force is None else force + t
                force = force * scales[pl.ds(start + sides, ROWS), :]
                total[2 * m + k] = force if i == 0 else total[2 * m + k] + force
    return [total[ch] for ch in range(6)]


def by_corner(stiff, e):
    return lambda k, i, m, c: stiff[3 * (4 * k + 2 * i + e) + m, c]


def first_kernel(stiff, owner, spread, from_left, from_right, above, below, u, v, mass, mod, ref, pair, vel, dis, weight, point, index, who, scale, at_left, at_right, at_edge):
    edges = edge_columns(
        extended(from_left[...], above[AT_L : AT_L + 1, :], below[AT_L : AT_L + 1, :]),
        extended(from_right[...], above[AT_R : AT_R + 1, :], below[AT_R : AT_R + 1, :]),
    )
    zero = jnp.zeros((8, COLS), F32)
    lane = lanes((16, COLS))
    for ch in range(8):
        at = AT_U + 2 * ch if ch < 6 else AT_E + 2 * (ch - 6)
        at_left[ch, 0:2, :] = above[at : at + 2, :]
        at_left[ch, 2:10, :] = u[ch // 2, ch % 2] if ch < 6 else mod[ch - 6]
        at_left[ch, 10:12, :] = below[at : at + 2, :]
        at_left[ch, 12:16, :] = zero[:4]
        side = edges[16 * ch : 16 * ch + 16, :]
        at_right[ch, 0:16, :] = with_columns(at_left[ch, 0:16, :], side)
        at_edge[ch, 0:16, :] = side
        for buf in (at_left, at_right, at_edge):
            buf[ch, 16:24, :] = zero
    here, right, side = [buf[6, 0:16, :] + buf[7, 0:16, :] for buf in (at_left, at_right, at_edge)]
    for n, both in enumerate((here + right, side + here)):
        scale[n, 0:16, :] = (both + pltpu.roll(both, 15, axis=0)) * 0.125
        scale[n, 16:24, :] = zero
    scale[2] = jnp.where(lanes((24, COLS)) < 64, scale[1], scale[0])
    for k in range(2):
        weight[k, 0:1, :] = above[AT_M + k : AT_M + k + 1, :]
        weight[k, 1:9, :] = mass[k]
        weight[k, 9:10, :] = below[AT_M + k : AT_M + k + 1, :]
        weight[k, 10:16, :] = jnp.ones((6, COLS), F32)
        weight[k] = DT / weight[k]
    for ch in range(6):
        vel[ch, 0:1, :] = above[AT_V + ch : AT_V + ch + 1, :]
        vel[ch, 1:9, :] = v[ch // 2, ch % 2]
        vel[ch, 9:10, :] = below[AT_V + ch : AT_V + ch + 1, :]
        vel[ch, 10:16, :] = zero[:6]
    for m in range(3):
        point[m, 0:1, :] = above[AT_X + m : AT_X + m + 1, :]
        point[m, 1:9, :] = ref[m]
        point[m, 9:10, :] = below[AT_X + m : AT_X + m + 1, :]
        point[m, 10:16, :] = zero[:6]
        point[m] = point[m] + at_left[2 * m, 1:17, :]
    index[0:1, :] = above[AT_P : AT_P + 1, :].astype(jnp.int32)
    index[1:9, :] = pair[0]
    index[9:10, :] = below[AT_P : AT_P + 1, :].astype(jnp.int32)
    index[10:16, :] = jnp.zeros((6, COLS), jnp.int32)
    who[...] = jnp.zeros((8, COLS), jnp.int32)
    who[0:1, :] = above[AT_O : AT_O + 1, :].astype(jnp.int32)
    who[1:2, :] = below[AT_O : AT_O + 1, :].astype(jnp.int32)
    for step in range(2):
        who[2 + step : 3 + step, 0:ROWS] = owner[step]
    del spread
    straight, moved, edge = {}, {}, {}
    for i in range(2):
        start = 1 - i
        s_main, s_edge = [scale[n, start : start + 16, :] for n in range(2)]
        for k in range(2):
            for m in range(3):
                sums = [None, None, None]
                for c, ch, x, e in corners():
                    rows = slice(start + x, start + x + 16)
                    near = at_left[ch, rows, :]
                    main, side = (at_right[ch, rows, :], near) if e else (near, at_edge[ch, rows, :])
                    w0, w1 = [stiff[3 * (4 * k + 2 * i + end) + m, c] for end in range(2)]
                    terms = (w0 * main, w1 * main, w1 * side)
                    sums = [t if s is None else s + t for s, t in zip(sums, terms)]
                for into, s, by in zip((straight, moved, edge), sums, (s_main, s_main, s_edge)):
                    into[2 * m + k] = s * by if i == 0 else into[2 * m + k] + s * by
    for ch in range(6):
        force = straight[ch] + jnp.where(lane == 0, edge[ch], pltpu.roll(moved[ch], 1, axis=1))
        new = vel[ch] - weight[ch % 2] * force
        vel[ch] = new
        dis[ch] = at_left[ch, 1:17, :] + DT * new


def spread_kernel(stiff, spread):
    lane = lanes((1, COLS))
    for k in range(2):
        for i in range(2):
            for m in range(3):
                for c in range(24):
                    one, other = [stiff[3 * (4 * k + 2 * i + e) + m, c] for e in (1, 0)]
                    at = 24 * (6 * k + 3 * i + m) + c
                    spread[at : at + 1, :] = jnp.where(lane < 64, one, other)


def look_up(table, owner, index, row, out):
    which = jnp.broadcast_to(index, (8, COLS))
    place, part = which & 127, (which >> 7) & 3
    found = None
    for c in range(4):
        got = jnp.take_along_axis(table[owner, 8 * c : 8 * c + 8, :], place, axis=1)
        found = got if found is None else jnp.where(part == c, got, found)
    found = jnp.where(which[0:4] >= 512, found[4:8], found[0:4])
    for c in range(4):
        out[c, row : row + 1, :] = found[c : c + 1]


def contact(words, points):
    depth = jnp.maximum(words[3] - (words[0] * points[0] + words[1] * points[1] + words[2] * points[2]), 0.0)
    return [words[m] * depth for m in range(3)]


def contact_kernel(who, table, index, vel, dis, weight, point, new_vel, new_dis, left, right, words, square):
    words[:, 8:16, :] = jnp.zeros((4, 8, COLS), F32)
    for b in range(ROWS + 2):
        look_up(table, who[0, ROWS - 1] if b == 0 else who[1, 0] if b == ROWS + 1 else who[2, b - 1], index[b : b + 1, :], b, words)
    pushes = contact([words[c] for c in range(4)], [point[m] for m in range(3)])
    for m in range(3):
        step = weight[0] * pushes[m]
        new_vel[2 * m] = (vel[2 * m] + step)[1:9]
        new_vel[2 * m + 1] = vel[2 * m + 1, 1:9, :]
        new_dis[2 * m] = dis[2 * m] + DT * step
        new_dis[2 * m + 1] = dis[2 * m + 1]
    for ch in range(6):
        square[16 * ch : 16 * ch + 16, :] = new_dis[ch]
    square[96:128, :] = jnp.zeros((32, COLS), F32)
    turned = jnp.transpose(square[...])
    left[...] = turned[0:1, :]
    right[...] = turned[COLS - 1 : COLS, :]


def inner_kernel(who, stiff, table, pair, dis, vel, mass, ref, scale, base_dis, base_vel, weight, at_right, words):
    lane = lanes((ROWS, COLS))
    for b in range(ROWS):
        look_up(table, who[3, b], pair[1, b : b + 1, :], b, words)
    push = contact([words[c] for c in range(4)], [ref[m] + dis[2 * m, 1:9, :] for m in range(3)])
    for ch in range(6):
        at_right[ch] = pltpu.roll(dis[ch], COLS - 1, axis=1)
    straight = element_sums(by_corner(stiff, 0), (dis, at_right), 1, scale.at[0], 0)
    moved = element_sums(by_corner(stiff, 1), (dis, at_right), 1, scale.at[0], 0)
    for k in range(2):
        weight[k] = DT / mass[k]
        for m in range(3):
            ch = 2 * m + k
            force = jnp.where(lane == COLS - 1, 0.0, straight[ch]) + jnp.where(lane == 0, 0.0, pltpu.roll(moved[ch], 1, axis=1))
            net = push[m] - force if k == 0 else -force
            new = vel[ch] + weight[k] * net
            base_vel[ch] = new
            base_dis[ch] = dis[ch, 1:9, :] + DT * new


def outer_kernel(dis, base_dis, base_vel, weight, scale, spread, from_left, from_right, out_dis, out_vel, at_left, at_right):
    edges = edge_columns(from_left[...], from_right[...])
    lane = lanes((16, COLS))
    for ch in range(6):
        here, side = dis[ch], edges[16 * ch : 16 * ch + 16, :]
        at_left[ch] = jnp.where(lane < 64, side, here)
        at_right[ch] = jnp.where(lane < 64, here, side)

    def spread_row(k, i, m, c):
        at = 24 * (6 * k + 3 * i + m) + c
        return spread[at : at + 1, :]

    forces = element_sums(spread_row, (at_left, at_right), 1, scale.at[2], 0)
    lane = lanes((ROWS, COLS))
    for m in range(3):
        for k in range(2):
            ch = 2 * m + k
            change = weight[k] * jnp.where((lane == 0) | (lane == COLS - 1), forces[ch], 0.0)
            out_vel[m, k] = base_vel[ch] - change
            out_dis[m, k] = base_dis[ch] - DT * change


def call(kernel, outs, specs, scratch=(), room=16, out_specs=None, flops=1_000_000, moved=1_000_000):
    return pl.pallas_call(
        kernel,
        out_shape=outs,
        in_specs=specs,
        out_specs=out_specs or jax.tree.map(lambda _: VMEM, outs),
        scratch_shapes=list(scratch),
        compiler_params=pltpu.CompilerParams(vmem_limit_bytes=room << 20),
        cost_estimate=pl.CostEstimate(flops=flops, bytes_accessed=moved, transcendentals=0),
    )


def swapped(to_next, to_last, axis):
    size = lax.axis_size(axis)
    up = [(i, (i + 1) % size) for i in range(size)]
    down = [(j, i) for i, j in up]
    return lax.ppermute(to_next, axis, up), lax.ppermute(to_last, axis, down)


def shards(u, v, mass, mod, stiff, ref, facets, penalty, owners, pair):
    width = facets.shape[-1]
    owner = owners.reshape(2, 1, ROWS)
    sources = (facets.reshape(6 * width // COLS, COLS), penalty.reshape(width // COLS, COLS))
    table = call(
        table_kernel,
        struct(OWNERS, 32, COLS),
        [HBM] * 2,
        [pltpu.VMEM(x.shape, x.dtype) for x in sources]
        + [pltpu.VMEM((REPLICAS, 32, COLS), F32)]
        + [pltpu.SemaphoreType.DMA((n,)) for n in (2, OWNERS // REPLICAS)],
        room=60,
        out_specs=HBM,
    )(*sources)
    left, right = call(
        columns_kernel, (struct(1, COLS), struct(1, COLS)), [VMEM] * 2, [pltpu.VMEM((128, COLS), F32)]
    )(u, mod)
    tables = lax.all_to_all(table, "mesh", split_axis=0, concat_axis=0, tiled=True)
    from_left, from_right = swapped(right, left, "sub")
    up, down = call(pack_kernel, (struct(MSG, COLS), struct(MSG, COLS)), [VMEM] * 9)(
        u, v, mass, mod, ref, pair, owner, from_left, from_right
    )
    above, below = swapped(down, up, "mesh")
    spread = call(spread_kernel, struct(288, COLS), [SMEM])(stiff)
    vel, dis, weight, point, index, who, scale = call(
        first_kernel,
        (
            struct(6, 16, COLS),
            struct(6, 16, COLS),
            struct(2, 16, COLS),
            struct(3, 16, COLS),
            struct(16, COLS, dtype=jnp.int32),
            struct(8, COLS, dtype=jnp.int32),
            struct(3, 24, COLS),
        ),
        [SMEM] + [VMEM] * 12,
        [pltpu.VMEM((8, 24, COLS), F32)] * 3,
    )(stiff, owner, spread, from_left, from_right, above, below, u, v, mass, mod, ref, pair)
    new_vel, new_dis, left, right = call(
        contact_kernel,
        (struct(6, ROWS, COLS), struct(6, 16, COLS), struct(1, COLS), struct(1, COLS)),
        [VMEM] * 7,
        [pltpu.VMEM((4, 16, COLS), F32), pltpu.VMEM((128, COLS), F32)],
    )(who, tables, index, vel, dis, weight, point)
    from_left, from_right = swapped(right, left, "sub")
    base_dis, base_vel, weight = call(
        inner_kernel,
        (struct(6, ROWS, COLS), struct(6, ROWS, COLS), struct(2, ROWS, COLS)),
        [VMEM, SMEM] + [VMEM] * 7,
        [pltpu.VMEM((6, 16, COLS), F32), pltpu.VMEM((4, 8, COLS), F32)],
    )(who, stiff, tables, pair, new_dis, new_vel, mass, ref, scale)
    return call(
        outer_kernel,
        (struct(3, 2, ROWS, COLS), struct(3, 2, ROWS, COLS)),
        [VMEM] * 8,
        [pltpu.VMEM((6, 16, COLS), F32)] * 2,
    )(new_dis, base_dis, base_vel, weight, scale, spread, from_left, from_right)


def solution(mesh):
    in_specs = (
        P(None, None, "mesh", "sub"),
        P(None, None, "mesh", "sub"),
        P(None, "mesh", "sub"),
        P(None, "mesh", "sub"),
        P(),
        P(None, "mesh", "sub"),
        P("mesh", "sub", None, None),
        P("mesh", "sub", None),
        P(None, "mesh", "sub", None, None),
        P(None, "mesh", "sub"),
    )
    out_specs = (P(None, None, "mesh", "sub"), P(None, None, "mesh", "sub"))
    return jax.shard_map(shards, mesh=mesh, in_specs=in_specs, out_specs=out_specs, check_vma=False)
```

```python
import jax
import jax.numpy as jnp
from jax import lax
from jax.experimental import pallas as pl
from jax.experimental.pallas import tpu as pltpu
from jax.sharding import PartitionSpec as P

DT = 0.1
F32 = jnp.float32
VMEM = pl.BlockSpec(memory_space=pltpu.VMEM)
HBM = pl.BlockSpec(memory_space=pltpu.HBM)
ROWS = 8
COLS = 128
OWNERS = 32
REPLICAS = 8
AT_U, AT_E, AT_V, AT_M, AT_X, AT_P, AT_O, AT_L, AT_R = 0, 12, 16, 22, 24, 27, 28, 29, 30
MSG = 32


def struct(*shape, dtype=F32):
    return jax.ShapeDtypeStruct(shape, dtype)


def lanes(shape):
    return lax.broadcasted_iota(jnp.int32, shape, len(shape) - 1)


def table_kernel(fac, pen, table, fac_, pen_, mine, sems, out_sems):
    copies = [pltpu.make_async_copy(a, b, sems.at[n]) for n, (a, b) in enumerate(((fac, fac_), (pen, pen_)))]
    for copy in copies:
        copy.start()
    for copy in copies:
        copy.wait()
    root = jnp.sqrt(pen_[...])
    c, n = [[fac_[8 * (m + at) : 8 * (m + at) + 8, :] for m in range(3)] for at in (0, 3)]
    dist = n[0] * c[0] + n[1] * c[1] + n[2] * c[2]
    words = [root * n[0], root * n[1], root * n[2], root * dist]
    for q in range(4):
        tile = jnp.concatenate([w[4 * h + q : 4 * h + q + 1, :] for h in range(2) for w in words], axis=0)
        for r in range(REPLICAS):
            mine[r, 8 * q : 8 * q + 8, :] = tile
    outs = [pltpu.make_async_copy(mine, table.at[pl.ds(o * REPLICAS, REPLICAS)], out_sems.at[o]) for o in range(OWNERS // REPLICAS)]
    for copy in outs:
        copy.start()
    for copy in outs:
        copy.wait()


def columns_kernel(u, mod, left, right, square):
    for ch in range(8):
        square[16 * ch : 16 * ch + 8, :] = u[ch // 2, ch % 2] if ch < 6 else mod[ch - 6]
        square[16 * ch + 8 : 16 * ch + 16, :] = jnp.zeros((8, COLS), F32)
    turned = jnp.transpose(square[...])
    left[...] = turned[0:1, :]
    right[...] = turned[COLS - 1 : COLS, :]


def pack_kernel(u, v, mass, mod, ref, pair, own, from_left, from_right, up, down):
    for out, two, one in ((down, ROWS - 2, ROWS - 1), (up, 0, 0)):
        for m in range(3):
            for k in range(2):
                ch = 2 * m + k
                out[AT_U + 2 * ch : AT_U + 2 * ch + 2, :] = u[m, k, two : two + 2, :]
                out[AT_V + ch : AT_V + ch + 1, :] = v[m, k, one : one + 1, :]
            out[AT_X + m : AT_X + m + 1, :] = ref[m, one : one + 1, :]
        for k in range(2):
            out[AT_E + 2 * k : AT_E + 2 * k + 2, :] = mod[k, two : two + 2, :]
            out[AT_M + k : AT_M + k + 1, :] = mass[k, one : one + 1, :]
        out[AT_P : AT_P + 1, :] = pair[0, one : one + 1, :].astype(F32)
        out[AT_O :, :] = jnp.zeros((MSG - AT_O, COLS), F32)
        out[AT_O : AT_O + 1, 0:ROWS] = own[0].astype(F32)
        out[AT_L : AT_L + 1, :] = from_left[...]
        out[AT_R : AT_R + 1, :] = from_right[...]


def extended(here, above, below):
    here, above, below = [jnp.broadcast_to(x, (8, COLS)) for x in (here, above, below)]
    at = lanes((8, COLS)) & 15
    out = jnp.where(at < 12, pltpu.roll(below, 10, axis=1), 0.0)
    out = jnp.where(at < 10, pltpu.roll(here, 2, axis=1), out)
    return jnp.where(at < 2, pltpu.roll(above, COLS - 6, axis=1), out)[0:1]


def edge_columns(from_left, from_right):
    sub = lax.broadcasted_iota(jnp.int32, (128, COLS), 0)
    both = jnp.where(sub < 64, jnp.broadcast_to(from_left, (128, COLS)), jnp.broadcast_to(from_right, (128, COLS)))
    return jnp.transpose(both)


def with_columns(here, edges):
    lane = lanes(here.shape)
    return jnp.where(lane == COLS - 1, edges, pltpu.roll(here, COLS - 1, axis=1))


def corners():
    return [(3 * (4 * k + 2 * x + e) + m, 2 * m + k, x, e) for k in range(2) for x in range(2) for e in range(2) for m in range(3)]


def element_sums(weight, rows_of, sides, scales, at):
    total = {}
    for i in range(2):
        start = at + 1 - i
        values = {c: rows_of[e][ch, pl.ds(start + x, ROWS), :] for c, ch, x, e in corners()}
        for k in range(2):
            for m in range(3):
                force = None
                for c in range(24):
                    t = weight(k, i, m, c) * values[c]
                    force = t if force is None else force + t
                force = force * scales[pl.ds(start + sides, ROWS), :]
                total[2 * m + k] = force if i == 0 else total[2 * m + k] + force
    return [total[ch] for ch in range(6)]


def by_corner(entries, e):
    return lambda k, i, m, c: entries[entry(k, i, e, m, c), :]


def entry(k, i, e, m, c):
    at = 24 * c + 3 * (4 * k + 2 * i + e) + m
    return slice(at, at + 1)


def first_kernel(entries, owner, from_left, from_right, above, below, u, v, mass, mod, ref, pair, vel, dis, weight, point, index, who, scale, at_left, at_right, at_edge):
    edges = edge_columns(
        extended(from_left[...], above[AT_L : AT_L + 1, :], below[AT_L : AT_L + 1, :]),
        extended(from_right[...], above[AT_R : AT_R + 1, :], below[AT_R : AT_R + 1, :]),
    )
    zero = jnp.zeros((8, COLS), F32)
    lane = lanes((16, COLS))
    for ch in range(8):
        at = AT_U + 2 * ch if ch < 6 else AT_E + 2 * (ch - 6)
        at_left[ch, 0:2, :] = above[at : at + 2, :]
        at_left[ch, 2:10, :] = u[ch // 2, ch % 2] if ch < 6 else mod[ch - 6]
        at_left[ch, 10:12, :] = below[at : at + 2, :]
        at_left[ch, 12:16, :] = zero[:4]
        side = edges[16 * ch : 16 * ch + 16, :]
        at_right[ch, 0:16, :] = with_columns(at_left[ch, 0:16, :], side)
        at_edge[ch, 0:16, :] = side
        for buf in (at_left, at_right, at_edge):
            buf[ch, 16:24, :] = zero
    here, right, side = [buf[6, 0:16, :] + buf[7, 0:16, :] for buf in (at_left, at_right, at_edge)]
    for n, both in enumerate((here + right, side + here)):
        scale[n, 0:16, :] = (both + pltpu.roll(both, 15, axis=0)) * 0.125
        scale[n, 16:24, :] = zero
    scale[2] = jnp.where(lanes((24, COLS)) < 64, scale[1], scale[0])
    for k in range(2):
        weight[k, 0:1, :] = above[AT_M + k : AT_M + k + 1, :]
        weight[k, 1:9, :] = mass[k]
        weight[k, 9:10, :] = below[AT_M + k : AT_M + k + 1, :]
        weight[k, 10:16, :] = jnp.ones((6, COLS), F32)
        weight[k] = DT / weight[k]
    for ch in range(6):
        vel[ch, 0:1, :] = above[AT_V + ch : AT_V + ch + 1, :]
        vel[ch, 1:9, :] = v[ch // 2, ch % 2]
        vel[ch, 9:10, :] = below[AT_V + ch : AT_V + ch + 1, :]
        vel[ch, 10:16, :] = zero[:6]
    for m in range(3):
        point[m, 0:1, :] = above[AT_X + m : AT_X + m + 1, :]
        point[m, 1:9, :] = ref[m]
        point[m, 9:10, :] = below[AT_X + m : AT_X + m + 1, :]
        point[m, 10:16, :] = zero[:6]
        point[m] = point[m] + at_left[2 * m, 1:17, :]
    index[0:1, :] = above[AT_P : AT_P + 1, :].astype(jnp.int32)
    index[1:9, :] = pair[0]
    index[9:10, :] = below[AT_P : AT_P + 1, :].astype(jnp.int32)
    index[10:16, :] = jnp.zeros((6, COLS), jnp.int32)
    who[...] = jnp.zeros((8, COLS), jnp.int32)
    who[0:1, :] = above[AT_O : AT_O + 1, :].astype(jnp.int32)
    who[1:2, :] = below[AT_O : AT_O + 1, :].astype(jnp.int32)
    for step in range(2):
        who[2 + step : 3 + step, 0:ROWS] = owner[step]
    straight, moved, edge = {}, {}, {}
    for i in range(2):
        start = 1 - i
        s_main, s_edge = [scale[n, start : start + 16, :] for n in range(2)]
        for k in range(2):
            for m in range(3):
                sums = [None, None, None]
                for c, ch, x, e in corners():
                    rows = slice(start + x, start + x + 16)
                    near = at_left[ch, rows, :]
                    main, side = (at_right[ch, rows, :], near) if e else (near, at_edge[ch, rows, :])
                    w0, w1 = [entries[entry(k, i, end, m, c), :] for end in range(2)]
                    terms = (w0 * main, w1 * main, w1 * side)
                    sums = [t if s is None else s + t for s, t in zip(sums, terms)]
                for into, s, by in zip((straight, moved, edge), sums, (s_main, s_main, s_edge)):
                    into[2 * m + k] = s * by if i == 0 else into[2 * m + k] + s * by
    for ch in range(6):
        force = straight[ch] + jnp.where(lane == 0, edge[ch], pltpu.roll(moved[ch], 1, axis=1))
        new = vel[ch] - weight[ch % 2] * force
        vel[ch] = new
        dis[ch] = at_left[ch, 1:17, :] + DT * new


def spread_kernel(stiff, entries, sided):
    lane = lanes((24, COLS))
    for c in range(24):
        column = jnp.broadcast_to(stiff[:, c : c + 1], (24, COLS))
        entries[24 * c : 24 * c + 24, :] = column
        sided[24 * c : 24 * c + 24, :] = jnp.where(lane < 64, pltpu.roll(column, 21, axis=0), column)


def look_up(table, owner, index, row, out):
    which = jnp.broadcast_to(index, (8, COLS))
    place, part = which & 127, (which >> 7) & 3
    found = None
    for c in range(4):
        got = jnp.take_along_axis(table[owner, 8 * c : 8 * c + 8, :], place, axis=1)
        found = got if found is None else jnp.where(part == c, got, found)
    found = jnp.where(which[0:4] >= 512, found[4:8], found[0:4])
    for c in range(4):
        out[c, row : row + 1, :] = found[c : c + 1]


def contact(words, points):
    depth = jnp.maximum(words[3] - (words[0] * points[0] + words[1] * points[1] + words[2] * points[2]), 0.0)
    return [words[m] * depth for m in range(3)]


def contact_kernel(who, table, index, vel, dis, weight, point, new_vel, new_dis, left, right, words, square):
    words[:, 8:16, :] = jnp.zeros((4, 8, COLS), F32)
    for b in range(ROWS + 2):
        look_up(table, who[0, ROWS - 1] if b == 0 else who[1, 0] if b == ROWS + 1 else who[2, b - 1], index[b : b + 1, :], b, words)
    pushes = contact([words[c] for c in range(4)], [point[m] for m in range(3)])
    for m in range(3):
        step = weight[0] * pushes[m]
        new_vel[2 * m] = (vel[2 * m] + step)[1:9]
        new_vel[2 * m + 1] = vel[2 * m + 1, 1:9, :]
        new_dis[2 * m] = dis[2 * m] + DT * step
        new_dis[2 * m + 1] = dis[2 * m + 1]
    for ch in range(6):
        square[16 * ch : 16 * ch + 16, :] = new_dis[ch]
    square[96:128, :] = jnp.zeros((32, COLS), F32)
    turned = jnp.transpose(square[...])
    left[...] = turned[0:1, :]
    right[...] = turned[COLS - 1 : COLS, :]


def inner_kernel(who, entries, table, pair, dis, vel, mass, ref, scale, base_dis, base_vel, weight, at_right, words):
    lane = lanes((ROWS, COLS))
    for b in range(ROWS):
        look_up(table, who[3, b], pair[1, b : b + 1, :], b, words)
    push = contact([words[c] for c in range(4)], [ref[m] + dis[2 * m, 1:9, :] for m in range(3)])
    for ch in range(6):
        at_right[ch] = pltpu.roll(dis[ch], COLS - 1, axis=1)
    straight = element_sums(by_corner(entries, 0), (dis, at_right), 1, scale.at[0], 0)
    moved = element_sums(by_corner(entries, 1), (dis, at_right), 1, scale.at[0], 0)
    for k in range(2):
        weight[k] = DT / mass[k]
        for m in range(3):
            ch = 2 * m + k
            force = jnp.where(lane == COLS - 1, 0.0, straight[ch]) + jnp.where(lane == 0, 0.0, pltpu.roll(moved[ch], 1, axis=1))
            net = push[m] - force if k == 0 else -force
            new = vel[ch] + weight[k] * net
            base_vel[ch] = new
            base_dis[ch] = dis[ch, 1:9, :] + DT * new


def outer_kernel(dis, base_dis, base_vel, weight, scale, sided, from_left, from_right, out_dis, out_vel, at_left, at_right):
    edges = edge_columns(from_left[...], from_right[...])
    lane = lanes((16, COLS))
    for ch in range(6):
        here, side = dis[ch], edges[16 * ch : 16 * ch + 16, :]
        at_left[ch] = jnp.where(lane < 64, side, here)
        at_right[ch] = jnp.where(lane < 64, here, side)

    forces = element_sums(by_corner(sided, 0), (at_left, at_right), 1, scale.at[2], 0)
    lane = lanes((ROWS, COLS))
    for m in range(3):
        for k in range(2):
            ch = 2 * m + k
            change = weight[k] * jnp.where((lane == 0) | (lane == COLS - 1), forces[ch], 0.0)
            out_vel[m, k] = base_vel[ch] - change
            out_dis[m, k] = base_dis[ch] - DT * change


def call(kernel, outs, specs, scratch=(), room=16, out_specs=None, flops=1_000_000, moved=1_000_000):
    return pl.pallas_call(
        kernel,
        out_shape=outs,
        in_specs=specs,
        out_specs=out_specs or jax.tree.map(lambda _: VMEM, outs),
        scratch_shapes=list(scratch),
        compiler_params=pltpu.CompilerParams(vmem_limit_bytes=room << 20),
        cost_estimate=pl.CostEstimate(flops=flops, bytes_accessed=moved, transcendentals=0),
    )


def swapped(to_next, to_last, axis):
    size = lax.axis_size(axis)
    up = [(i, (i + 1) % size) for i in range(size)]
    down = [(j, i) for i, j in up]
    return lax.ppermute(to_next, axis, up), lax.ppermute(to_last, axis, down)


def shards(u, v, mass, mod, stiff, ref, facets, penalty, owners, pair):
    width = facets.shape[-1]
    owner = owners.reshape(2, 1, ROWS)
    sources = (facets.reshape(6 * width // COLS, COLS), penalty.reshape(width // COLS, COLS))
    table = call(
        table_kernel,
        struct(OWNERS, 32, COLS),
        [HBM] * 2,
        [pltpu.VMEM(x.shape, x.dtype) for x in sources]
        + [pltpu.VMEM((REPLICAS, 32, COLS), F32)]
        + [pltpu.SemaphoreType.DMA((n,)) for n in (2, OWNERS // REPLICAS)],
        room=60,
        out_specs=HBM,
    )(*sources)
    left, right = call(
        columns_kernel, (struct(1, COLS), struct(1, COLS)), [VMEM] * 2, [pltpu.VMEM((128, COLS), F32)]
    )(u, mod)
    tables = lax.all_to_all(table, "mesh", split_axis=0, concat_axis=0, tiled=True)
    from_left, from_right = swapped(right, left, "sub")
    up, down = call(pack_kernel, (struct(MSG, COLS), struct(MSG, COLS)), [VMEM] * 9)(
        u, v, mass, mod, ref, pair, owner, from_left, from_right
    )
    above, below = swapped(down, up, "mesh")
    entries, sided = call(spread_kernel, (struct(576, COLS), struct(576, COLS)), [VMEM])(stiff)
    vel, dis, weight, point, index, who, scale = call(
        first_kernel,
        (
            struct(6, 16, COLS),
            struct(6, 16, COLS),
            struct(2, 16, COLS),
            struct(3, 16, COLS),
            struct(16, COLS, dtype=jnp.int32),
            struct(8, COLS, dtype=jnp.int32),
            struct(3, 24, COLS),
        ),
        [VMEM] * 12,
        [pltpu.VMEM((8, 24, COLS), F32)] * 3,
    )(entries, owner, from_left, from_right, above, below, u, v, mass, mod, ref, pair)
    new_vel, new_dis, left, right = call(
        contact_kernel,
        (struct(6, ROWS, COLS), struct(6, 16, COLS), struct(1, COLS), struct(1, COLS)),
        [VMEM] * 7,
        [pltpu.VMEM((4, 16, COLS), F32), pltpu.VMEM((128, COLS), F32)],
    )(who, tables, index, vel, dis, weight, point)
    from_left, from_right = swapped(right, left, "sub")
    base_dis, base_vel, weight = call(
        inner_kernel,
        (struct(6, ROWS, COLS), struct(6, ROWS, COLS), struct(2, ROWS, COLS)),
        [VMEM] * 9,
        [pltpu.VMEM((6, 16, COLS), F32), pltpu.VMEM((4, 8, COLS), F32)],
    )(who, entries, tables, pair, new_dis, new_vel, mass, ref, scale)
    return call(
        outer_kernel,
        (struct(3, 2, ROWS, COLS), struct(3, 2, ROWS, COLS)),
        [VMEM] * 8,
        [pltpu.VMEM((6, 16, COLS), F32)] * 2,
    )(new_dis, base_dis, base_vel, weight, scale, sided, from_left, from_right)


def solution(mesh):
    in_specs = (
        P(None, None, "mesh", "sub"),
        P(None, None, "mesh", "sub"),
        P(None, "mesh", "sub"),
        P(None, "mesh", "sub"),
        P(),
        P(None, "mesh", "sub"),
        P("mesh", "sub", None, None),
        P("mesh", "sub", None),
        P(None, "mesh", "sub", None, None),
        P(None, "mesh", "sub"),
    )
    out_specs = (P(None, None, "mesh", "sub"), P(None, None, "mesh", "sub"))
    return jax.shard_map(shards, mesh=mesh, in_specs=in_specs, out_specs=out_specs, check_vma=False)
```

```python
import jax
import jax.numpy as jnp
from jax import lax
from jax.experimental import pallas as pl
from jax.experimental.pallas import tpu as pltpu
from jax.sharding import PartitionSpec as P

DT = 0.1
F32 = jnp.float32
VMEM = pl.BlockSpec(memory_space=pltpu.VMEM)
HBM = pl.BlockSpec(memory_space=pltpu.HBM)
ROWS = 8
COLS = 128
OWNERS = 32
REPLICAS = 8
AT_U, AT_E, AT_V, AT_M, AT_X, AT_P, AT_O = 0, 12, 16, 22, 24, 27, 28
MSG = 32


def struct(*shape, dtype=F32):
    return jax.ShapeDtypeStruct(shape, dtype)


def lanes(shape):
    return lax.broadcasted_iota(jnp.int32, shape, len(shape) - 1)


def pack_kernel(fac, pen, u, v, mass, mod, ref, pair, own, table, message, *held):
    held, mine, sems, out_sems = held[:-3], *held[-3:]
    copies = [pltpu.make_async_copy(a, b, sems.at[n]) for n, (a, b) in enumerate(zip((fac, pen, u, v, mass, mod, ref, pair, own), held))]
    for copy in copies:
        copy.start()
    fac, pen, u, v, mass, mod, ref, pair, own = held
    for copy in copies[:2]:
        copy.wait()
    root = jnp.sqrt(pen[...])
    c, n = [[fac[8 * (m + at) : 8 * (m + at) + 8, :] for m in range(3)] for at in (0, 3)]
    dist = n[0] * c[0] + n[1] * c[1] + n[2] * c[2]
    words = [root * n[0], root * n[1], root * n[2], root * dist]
    for q in range(4):
        tile = jnp.concatenate([w[4 * h + q : 4 * h + q + 1, :] for h in range(2) for w in words], axis=0)
        for r in range(REPLICAS):
            mine[r, 8 * q : 8 * q + 8, :] = tile
    outs = [pltpu.make_async_copy(mine, table.at[pl.ds(o * REPLICAS, REPLICAS)], out_sems.at[o]) for o in range(OWNERS // REPLICAS)]
    for copy in outs:
        copy.start()
    for copy in copies[2:]:
        copy.wait()
    for base, two, one in ((0, 0, 0), (MSG, ROWS - 2, ROWS - 1)):
        out = message.at[base : base + MSG]
        for m in range(3):
            for k in range(2):
                ch = 2 * m + k
                out[AT_U + 2 * ch : AT_U + 2 * ch + 2, :] = u[m, k, two : two + 2, :]
                out[AT_V + ch : AT_V + ch + 1, :] = v[m, k, one : one + 1, :]
            out[AT_X + m : AT_X + m + 1, :] = ref[m, one : one + 1, :]
        for k in range(2):
            out[AT_E + 2 * k : AT_E + 2 * k + 2, :] = mod[k, two : two + 2, :]
            out[AT_M + k : AT_M + k + 1, :] = mass[k, one : one + 1, :]
        out[AT_P : AT_P + 1, :] = pair[0, one : one + 1, :].astype(F32)
        out[AT_O :, :] = jnp.zeros((MSG - AT_O, COLS), F32)
        out[AT_O : AT_O + 1, 0:ROWS] = own[0].astype(F32)
    for copy in outs:
        copy.wait()


def extend_kernel(odd, first, other, u, mod, above, below, ext, left, right):
    here = odd[...] == 1
    above[...] = jnp.where(here, first[0, MSG:, :], other[0, MSG:, :])
    below[...] = jnp.where(here, other[1, :MSG, :], first[1, :MSG, :])
    for ch in range(8):
        at = AT_U + 2 * ch if ch < 6 else AT_E + 2 * (ch - 6)
        ext[16 * ch : 16 * ch + 2, :] = above[at : at + 2, :]
        ext[16 * ch + 2 : 16 * ch + 10, :] = u[ch // 2, ch % 2] if ch < 6 else mod[ch - 6]
        ext[16 * ch + 10 : 16 * ch + 12, :] = below[at : at + 2, :]
        ext[16 * ch + 12 : 16 * ch + 16, :] = jnp.zeros((4, COLS), F32)
    turned = jnp.transpose(ext[...])
    left[...] = turned[0:1, :]
    right[...] = turned[COLS - 1 : COLS, :]


def edge_columns(from_left, from_right):
    sub = lax.broadcasted_iota(jnp.int32, (128, COLS), 0)
    both = jnp.where(sub < 64, jnp.broadcast_to(from_left, (128, COLS)), jnp.broadcast_to(from_right, (128, COLS)))
    return jnp.transpose(both)


def with_columns(here, edges):
    lane = lanes(here.shape)
    return jnp.where(lane == COLS - 1, edges, pltpu.roll(here, COLS - 1, axis=1))


def corners():
    return [(3 * (4 * k + 2 * x + e) + m, 2 * m + k, x, e) for k in range(2) for x in range(2) for e in range(2) for m in range(3)]


def element_sums(weight, rows_of, sides, scales, at):
    total = {}
    for i in range(2):
        start = at + 1 - i
        values = {c: rows_of[e][ch, pl.ds(start + x, ROWS), :] for c, ch, x, e in corners()}
        for k in range(2):
            for m in range(3):
                force = None
                for c in range(24):
                    t = weight(k, i, m, c) * values[c]
                    force = t if force is None else force + t
                force = force * scales[pl.ds(start + sides, ROWS), :]
                total[2 * m + k] = force if i == 0 else total[2 * m + k] + force
    return [total[ch] for ch in range(6)]


def by_corner(entries, e):
    return lambda k, i, m, c: entries[entry(k, i, e, m, c), :]


def entry(k, i, e, m, c):
    at = 24 * c + 3 * (4 * k + 2 * i + e) + m
    return slice(at, at + 1)


def first_kernel(entries, owner, from_left, from_right, above, below, ext, v, mass, ref, pair, vel, dis, weight, point, index, who, scale, at_left, at_right, at_edge):
    edges = edge_columns(from_left[...], from_right[...])
    zero = jnp.zeros((8, COLS), F32)
    lane = lanes((16, COLS))
    for ch in range(8):
        here, side = ext[16 * ch : 16 * ch + 16, :], edges[16 * ch : 16 * ch + 16, :]
        at_left[ch, 0:16, :] = here
        at_right[ch, 0:16, :] = with_columns(here, side)
        at_edge[ch, 0:16, :] = side
        for buf in (at_left, at_right, at_edge):
            buf[ch, 16:24, :] = zero
    here, right, side = [buf[6, 0:16, :] + buf[7, 0:16, :] for buf in (at_left, at_right, at_edge)]
    for n, both in enumerate((here + right, side + here)):
        scale[n, 0:16, :] = (both + pltpu.roll(both, 15, axis=0)) * 0.125
        scale[n, 16:24, :] = zero
    scale[2] = jnp.where(lanes((24, COLS)) < 64, scale[1], scale[0])
    for k in range(2):
        weight[k, 0:1, :] = above[AT_M + k : AT_M + k + 1, :]
        weight[k, 1:9, :] = mass[k]
        weight[k, 9:10, :] = below[AT_M + k : AT_M + k + 1, :]
        weight[k, 10:16, :] = jnp.ones((6, COLS), F32)
        weight[k] = DT / weight[k]
    for ch in range(6):
        vel[ch, 0:1, :] = above[AT_V + ch : AT_V + ch + 1, :]
        vel[ch, 1:9, :] = v[ch // 2, ch % 2]
        vel[ch, 9:10, :] = below[AT_V + ch : AT_V + ch + 1, :]
        vel[ch, 10:16, :] = zero[:6]
    for m in range(3):
        point[m, 0:1, :] = above[AT_X + m : AT_X + m + 1, :]
        point[m, 1:9, :] = ref[m]
        point[m, 9:10, :] = below[AT_X + m : AT_X + m + 1, :]
        point[m, 10:16, :] = zero[:6]
        point[m] = point[m] + at_left[2 * m, 1:17, :]
    index[0:1, :] = above[AT_P : AT_P + 1, :].astype(jnp.int32)
    index[1:9, :] = pair[0]
    index[9:10, :] = below[AT_P : AT_P + 1, :].astype(jnp.int32)
    index[10:16, :] = jnp.zeros((6, COLS), jnp.int32)
    who[...] = jnp.zeros((8, COLS), jnp.int32)
    who[0:1, :] = above[AT_O : AT_O + 1, :].astype(jnp.int32)
    who[1:2, :] = below[AT_O : AT_O + 1, :].astype(jnp.int32)
    for step in range(2):
        who[2 + step : 3 + step, 0:ROWS] = owner[step]
    straight, moved, edge = {}, {}, {}
    for i in range(2):
        start = 1 - i
        s_main, s_edge = [scale[n, start : start + 16, :] for n in range(2)]
        for k in range(2):
            for m in range(3):
                sums = [None, None, None]
                for c, ch, x, e in corners():
                    rows = slice(start + x, start + x + 16)
                    near = at_left[ch, rows, :]
                    main, side = (at_right[ch, rows, :], near) if e else (near, at_edge[ch, rows, :])
                    w0, w1 = [entries[entry(k, i, end, m, c), :] for end in range(2)]
                    terms = (w0 * main, w1 * main, w1 * side)
                    sums = [t if s is None else s + t for s, t in zip(sums, terms)]
                for into, s, by in zip((straight, moved, edge), sums, (s_main, s_main, s_edge)):
                    into[2 * m + k] = s * by if i == 0 else into[2 * m + k] + s * by
    for ch in range(6):
        force = straight[ch] + jnp.where(lane == 0, edge[ch], pltpu.roll(moved[ch], 1, axis=1))
        new = vel[ch] - weight[ch % 2] * force
        vel[ch] = new
        dis[ch] = at_left[ch, 1:17, :] + DT * new


def spread_kernel(stiff, entries, sided):
    lane = lanes((24, COLS))
    for c in range(24):
        column = jnp.broadcast_to(stiff[:, c : c + 1], (24, COLS))
        entries[24 * c : 24 * c + 24, :] = column
        sided[24 * c : 24 * c + 24, :] = jnp.where(lane < 64, pltpu.roll(column, 21, axis=0), column)


def look_up(table, owner, index, row, out):
    which = jnp.broadcast_to(index, (8, COLS))
    place, part = which & 127, (which >> 7) & 3
    found = None
    for c in range(4):
        got = jnp.take_along_axis(table[owner, 8 * c : 8 * c + 8, :], place, axis=1)
        found = got if found is None else jnp.where(part == c, got, found)
    found = jnp.where(which[0:4] >= 512, found[4:8], found[0:4])
    for c in range(4):
        out[c, row : row + 1, :] = found[c : c + 1]


def contact(words, points):
    depth = jnp.maximum(words[3] - (words[0] * points[0] + words[1] * points[1] + words[2] * points[2]), 0.0)
    return [words[m] * depth for m in range(3)]


def contact_kernel(who, table, index, vel, dis, weight, point, new_vel, new_dis, left, right, words, square):
    words[:, 8:16, :] = jnp.zeros((4, 8, COLS), F32)
    for b in range(ROWS + 2):
        look_up(table, who[0, ROWS - 1] if b == 0 else who[1, 0] if b == ROWS + 1 else who[2, b - 1], index[b : b + 1, :], b, words)
    pushes = contact([words[c] for c in range(4)], [point[m] for m in range(3)])
    for m in range(3):
        step = weight[0] * pushes[m]
        new_vel[2 * m] = (vel[2 * m] + step)[1:9]
        new_vel[2 * m + 1] = vel[2 * m + 1, 1:9, :]
        new_dis[2 * m] = dis[2 * m] + DT * step
        new_dis[2 * m + 1] = dis[2 * m + 1]
    for ch in range(6):
        square[16 * ch : 16 * ch + 16, :] = new_dis[ch]
    square[96:128, :] = jnp.zeros((32, COLS), F32)
    turned = jnp.transpose(square[...])
    left[...] = turned[0:1, :]
    right[...] = turned[COLS - 1 : COLS, :]


def inner_kernel(who, entries, table, pair, dis, vel, mass, ref, scale, base_dis, base_vel, weight, at_right, words):
    lane = lanes((ROWS, COLS))
    for b in range(ROWS):
        look_up(table, who[3, b], pair[1, b : b + 1, :], b, words)
    push = contact([words[c] for c in range(4)], [ref[m] + dis[2 * m, 1:9, :] for m in range(3)])
    for ch in range(6):
        at_right[ch] = pltpu.roll(dis[ch], COLS - 1, axis=1)
    straight = element_sums(by_corner(entries, 0), (dis, at_right), 1, scale.at[0], 0)
    moved = element_sums(by_corner(entries, 1), (dis, at_right), 1, scale.at[0], 0)
    for k in range(2):
        weight[k] = DT / mass[k]
        for m in range(3):
            ch = 2 * m + k
            force = jnp.where(lane == COLS - 1, 0.0, straight[ch]) + jnp.where(lane == 0, 0.0, pltpu.roll(moved[ch], 1, axis=1))
            net = push[m] - force if k == 0 else -force
            new = vel[ch] + weight[k] * net
            base_vel[ch] = new
            base_dis[ch] = dis[ch, 1:9, :] + DT * new


def outer_kernel(dis, base_dis, base_vel, weight, scale, sided, from_left, from_right, out_dis, out_vel, at_left, at_right):
    edges = edge_columns(from_left[...], from_right[...])
    lane = lanes((16, COLS))
    for ch in range(6):
        here, side = dis[ch], edges[16 * ch : 16 * ch + 16, :]
        at_left[ch] = jnp.where(lane < 64, side, here)
        at_right[ch] = jnp.where(lane < 64, here, side)

    forces = element_sums(by_corner(sided, 0), (at_left, at_right), 1, scale.at[2], 0)
    lane = lanes((ROWS, COLS))
    for m in range(3):
        for k in range(2):
            ch = 2 * m + k
            change = weight[k] * jnp.where((lane == 0) | (lane == COLS - 1), forces[ch], 0.0)
            out_vel[m, k] = base_vel[ch] - change
            out_dis[m, k] = base_dis[ch] - DT * change


def call(kernel, outs, specs, scratch=(), room=16, out_specs=None, flops=1_000_000, moved=1_000_000):
    return pl.pallas_call(
        kernel,
        out_shape=outs,
        in_specs=specs,
        out_specs=out_specs or jax.tree.map(lambda _: VMEM, outs),
        scratch_shapes=list(scratch),
        compiler_params=pltpu.CompilerParams(vmem_limit_bytes=room << 20),
        cost_estimate=pl.CostEstimate(flops=flops, bytes_accessed=moved, transcendentals=0),
    )


def swapped(to_next, to_last, axis):
    size = lax.axis_size(axis)
    up = [(i, (i + 1) % size) for i in range(size)]
    down = [(j, i) for i, j in up]
    return lax.ppermute(to_next, axis, up), lax.ppermute(to_last, axis, down)


def shards(u, v, mass, mod, stiff, ref, facets, penalty, owners, pair):
    width = facets.shape[-1]
    owner = owners.reshape(2, 1, ROWS)
    sources = (
        facets.reshape(6 * width // COLS, COLS),
        penalty.reshape(width // COLS, COLS),
        *(u, v, mass, mod, ref, pair, owner),
    )
    table, message = call(
        pack_kernel,
        (struct(OWNERS, 32, COLS), struct(2 * MSG, COLS)),
        [HBM] * len(sources),
        [pltpu.VMEM(x.shape, x.dtype) for x in sources]
        + [pltpu.VMEM((REPLICAS, 32, COLS), F32)]
        + [pltpu.SemaphoreType.DMA((n,)) for n in (len(sources), OWNERS // REPLICAS)],
        room=60,
        out_specs=(HBM, VMEM),
    )(*sources)
    size = lax.axis_size("mesh")
    pairs = [[[i, (i + 1) % size] for i in range(start, size, 2)] for start in range(2)]
    first, other = [lax.all_gather(message, "mesh", axis_index_groups=groups) for groups in pairs]
    tables = lax.all_to_all(table, "mesh", split_axis=0, concat_axis=0, tiled=True)
    odd = jnp.full((1, COLS), lax.axis_index("mesh") % 2, jnp.int32)
    above, below, ext, left, right = call(
        extend_kernel,
        (struct(MSG, COLS), struct(MSG, COLS), struct(128, COLS), struct(1, COLS), struct(1, COLS)),
        [VMEM] * 5,
    )(odd, first, other, u, mod)
    from_left, from_right = swapped(right, left, "sub")
    entries, sided = call(spread_kernel, (struct(576, COLS), struct(576, COLS)), [VMEM])(stiff)
    vel, dis, weight, point, index, who, scale = call(
        first_kernel,
        (
            struct(6, 16, COLS),
            struct(6, 16, COLS),
            struct(2, 16, COLS),
            struct(3, 16, COLS),
            struct(16, COLS, dtype=jnp.int32),
            struct(8, COLS, dtype=jnp.int32),
            struct(3, 24, COLS),
        ),
        [VMEM] * 11,
        [pltpu.VMEM((8, 24, COLS), F32)] * 3,
    )(entries, owner, from_left, from_right, above, below, ext, v, mass, ref, pair)
    new_vel, new_dis, left, right = call(
        contact_kernel,
        (struct(6, ROWS, COLS), struct(6, 16, COLS), struct(1, COLS), struct(1, COLS)),
        [VMEM] * 7,
        [pltpu.VMEM((4, 16, COLS), F32), pltpu.VMEM((128, COLS), F32)],
    )(who, tables, index, vel, dis, weight, point)
    from_left, from_right = swapped(right, left, "sub")
    base_dis, base_vel, weight = call(
        inner_kernel,
        (struct(6, ROWS, COLS), struct(6, ROWS, COLS), struct(2, ROWS, COLS)),
        [VMEM] * 9,
        [pltpu.VMEM((6, 16, COLS), F32), pltpu.VMEM((4, 8, COLS), F32)],
    )(who, entries, tables, pair, new_dis, new_vel, mass, ref, scale)
    return call(
        outer_kernel,
        (struct(3, 2, ROWS, COLS), struct(3, 2, ROWS, COLS)),
        [VMEM] * 8,
        [pltpu.VMEM((6, 16, COLS), F32)] * 2,
    )(new_dis, base_dis, base_vel, weight, scale, sided, from_left, from_right)


def solution(mesh):
    in_specs = (
        P(None, None, "mesh", "sub"),
        P(None, None, "mesh", "sub"),
        P(None, "mesh", "sub"),
        P(None, "mesh", "sub"),
        P(),
        P(None, "mesh", "sub"),
        P("mesh", "sub", None, None),
        P("mesh", "sub", None),
        P(None, "mesh", "sub", None, None),
        P(None, "mesh", "sub"),
    )
    out_specs = (P(None, None, "mesh", "sub"), P(None, None, "mesh", "sub"))
    return jax.shard_map(shards, mesh=mesh, in_specs=in_specs, out_specs=out_specs, check_vma=False)
```

```python
import jax
import jax.numpy as jnp
from jax import lax
from jax.experimental import pallas as pl
from jax.experimental.pallas import tpu as pltpu
from jax.sharding import PartitionSpec as P

DT = 0.1
F32 = jnp.float32
VMEM = pl.BlockSpec(memory_space=pltpu.VMEM)
HBM = pl.BlockSpec(memory_space=pltpu.HBM)
ROWS = 8
COLS = 128
OWNERS = 32
REPLICAS = 8
AT_U, AT_E, AT_V, AT_M, AT_X, AT_P, AT_O, AT_L, AT_R = 0, 12, 16, 22, 24, 27, 28, 29, 30
MSG = 32


def struct(*shape, dtype=F32):
    return jax.ShapeDtypeStruct(shape, dtype)


def lanes(shape):
    return lax.broadcasted_iota(jnp.int32, shape, len(shape) - 1)


def table_kernel(fac, pen, table, fac_, pen_, mine, sems, out_sems):
    copies = [pltpu.make_async_copy(a, b, sems.at[n]) for n, (a, b) in enumerate(((fac, fac_), (pen, pen_)))]
    for copy in copies:
        copy.start()
    for copy in copies:
        copy.wait()
    root = jnp.sqrt(pen_[...])
    c, n = [[fac_[8 * (m + at) : 8 * (m + at) + 8, :] for m in range(3)] for at in (0, 3)]
    dist = n[0] * c[0] + n[1] * c[1] + n[2] * c[2]
    words = [root * n[0], root * n[1], root * n[2], root * dist]
    for q in range(4):
        tile = jnp.concatenate([w[4 * h + q : 4 * h + q + 1, :] for h in range(2) for w in words], axis=0)
        for r in range(REPLICAS):
            mine[r, 8 * q : 8 * q + 8, :] = tile
    outs = [pltpu.make_async_copy(mine, table.at[pl.ds(o * REPLICAS, REPLICAS)], out_sems.at[o]) for o in range(OWNERS // REPLICAS)]
    for copy in outs:
        copy.start()
    for copy in outs:
        copy.wait()


def columns_kernel(u, mod, left, right, square):
    for ch in range(8):
        square[16 * ch : 16 * ch + 8, :] = u[ch // 2, ch % 2] if ch < 6 else mod[ch - 6]
        square[16 * ch + 8 : 16 * ch + 16, :] = jnp.zeros((8, COLS), F32)
    turned = jnp.transpose(square[...])
    left[...] = turned[0:1, :]
    right[...] = turned[COLS - 1 : COLS, :]


def pack_kernel(u, v, mass, mod, ref, pair, own, from_left, from_right, up, down):
    for out, two, one in ((down, ROWS - 2, ROWS - 1), (up, 0, 0)):
        for m in range(3):
            for k in range(2):
                ch = 2 * m + k
                out[AT_U + 2 * ch : AT_U + 2 * ch + 2, :] = u[m, k, two : two + 2, :]
                out[AT_V + ch : AT_V + ch + 1, :] = v[m, k, one : one + 1, :]
            out[AT_X + m : AT_X + m + 1, :] = ref[m, one : one + 1, :]
        for k in range(2):
            out[AT_E + 2 * k : AT_E + 2 * k + 2, :] = mod[k, two : two + 2, :]
            out[AT_M + k : AT_M + k + 1, :] = mass[k, one : one + 1, :]
        out[AT_P : AT_P + 1, :] = pair[0, one : one + 1, :].astype(F32)
        out[AT_O :, :] = jnp.zeros((MSG - AT_O, COLS), F32)
        out[AT_O : AT_O + 1, 0:ROWS] = own[0].astype(F32)
        out[AT_L : AT_L + 1, :] = from_left[...]
        out[AT_R : AT_R + 1, :] = from_right[...]


def extended(here, above, below):
    here, above, below = [jnp.broadcast_to(x, (8, COLS)) for x in (here, above, below)]
    at = lanes((8, COLS)) & 15
    out = jnp.where(at < 12, pltpu.roll(below, 10, axis=1), 0.0)
    out = jnp.where(at < 10, pltpu.roll(here, 2, axis=1), out)
    return jnp.where(at < 2, pltpu.roll(above, COLS - 6, axis=1), out)[0:1]


def edge_columns(from_left, from_right):
    sub = lax.broadcasted_iota(jnp.int32, (128, COLS), 0)
    both = jnp.where(sub < 64, jnp.broadcast_to(from_left, (128, COLS)), jnp.broadcast_to(from_right, (128, COLS)))
    return jnp.transpose(both)


def with_columns(here, edges):
    lane = lanes(here.shape)
    return jnp.where(lane == COLS - 1, edges, pltpu.roll(here, COLS - 1, axis=1))


def corners():
    return [(3 * (4 * k + 2 * x + e) + m, 2 * m + k, x, e) for k in range(2) for x in range(2) for e in range(2) for m in range(3)]


def element_sums(weight, rows_of, sides, scales, at, ends=(0, 1)):
    total = {}
    for i in range(2):
        start = at + 1 - i
        values = {c: rows_of[e][ch, pl.ds(start + x, ROWS), :] for c, ch, x, e in corners() if e in ends}
        for k in range(2):
            for m in range(3):
                force = None
                for c in values:
                    t = weight(k, i, m, c) * values[c]
                    force = t if force is None else force + t
                force = force * scales[pl.ds(start + sides, ROWS), :]
                total[2 * m + k] = force if i == 0 else total[2 * m + k] + force
    return [total[ch] for ch in range(6)]


def by_corner(entries, e):
    return lambda k, i, m, c: entries[entry(k, i, e, m, c), :]


def entry(k, i, e, m, c):
    at = 24 * c + 3 * (4 * k + 2 * i + e) + m
    return slice(at, at + 1)


def first_kernel(entries, owner, from_left, from_right, above, below, u, v, mass, mod, ref, pair, vel, dis, weight, point, index, who, scale, at_left, at_right, at_edge):
    edges = edge_columns(
        extended(from_left[...], above[AT_L : AT_L + 1, :], below[AT_L : AT_L + 1, :]),
        extended(from_right[...], above[AT_R : AT_R + 1, :], below[AT_R : AT_R + 1, :]),
    )
    zero = jnp.zeros((8, COLS), F32)
    lane = lanes((16, COLS))
    for ch in range(8):
        at = AT_U + 2 * ch if ch < 6 else AT_E + 2 * (ch - 6)
        at_left[ch, 0:2, :] = above[at : at + 2, :]
        at_left[ch, 2:10, :] = u[ch // 2, ch % 2] if ch < 6 else mod[ch - 6]
        at_left[ch, 10:12, :] = below[at : at + 2, :]
        at_left[ch, 12:16, :] = zero[:4]
        side = edges[16 * ch : 16 * ch + 16, :]
        at_right[ch, 0:16, :] = with_columns(at_left[ch, 0:16, :], side)
        at_edge[ch, 0:16, :] = side
        for buf in (at_left, at_right, at_edge):
            buf[ch, 16:24, :] = zero
    here, right, side = [buf[6, 0:16, :] + buf[7, 0:16, :] for buf in (at_left, at_right, at_edge)]
    for n, both in enumerate((here + right, side + here)):
        scale[n, 0:16, :] = (both + pltpu.roll(both, 15, axis=0)) * 0.125
        scale[n, 16:24, :] = zero
    scale[2] = jnp.where(lanes((24, COLS)) < 64, scale[1], scale[0])
    for k in range(2):
        weight[k, 0:1, :] = above[AT_M + k : AT_M + k + 1, :]
        weight[k, 1:9, :] = mass[k]
        weight[k, 9:10, :] = below[AT_M + k : AT_M + k + 1, :]
        weight[k, 10:16, :] = jnp.ones((6, COLS), F32)
        weight[k] = DT / weight[k]
    for ch in range(6):
        vel[ch, 0:1, :] = above[AT_V + ch : AT_V + ch + 1, :]
        vel[ch, 1:9, :] = v[ch // 2, ch % 2]
        vel[ch, 9:10, :] = below[AT_V + ch : AT_V + ch + 1, :]
        vel[ch, 10:16, :] = zero[:6]
    for m in range(3):
        point[m, 0:1, :] = above[AT_X + m : AT_X + m + 1, :]
        point[m, 1:9, :] = ref[m]
        point[m, 9:10, :] = below[AT_X + m : AT_X + m + 1, :]
        point[m, 10:16, :] = zero[:6]
        point[m] = point[m] + at_left[2 * m, 1:17, :]
    index[0:1, :] = above[AT_P : AT_P + 1, :].astype(jnp.int32)
    index[1:9, :] = pair[0]
    index[9:10, :] = below[AT_P : AT_P + 1, :].astype(jnp.int32)
    index[10:16, :] = jnp.zeros((6, COLS), jnp.int32)
    who[...] = jnp.zeros((8, COLS), jnp.int32)
    who[0:1, :] = above[AT_O : AT_O + 1, :].astype(jnp.int32)
    who[1:2, :] = below[AT_O : AT_O + 1, :].astype(jnp.int32)
    for step in range(2):
        who[2 + step : 3 + step, 0:ROWS] = owner[step]
    straight, moved, edge = {}, {}, {}
    for i in range(2):
        start = 1 - i
        s_main, s_edge = [scale[n, start : start + 16, :] for n in range(2)]
        for k in range(2):
            for m in range(3):
                sums = [None, None, None]
                for c, ch, x, e in corners():
                    rows = slice(start + x, start + x + 16)
                    near = at_left[ch, rows, :]
                    main, side = (at_right[ch, rows, :], near) if e else (near, at_edge[ch, rows, :])
                    w0, w1 = [entries[entry(k, i, end, m, c), :] for end in range(2)]
                    terms = (w0 * main, w1 * main, w1 * side)
                    sums = [t if s is None else s + t for s, t in zip(sums, terms)]
                for into, s, by in zip((straight, moved, edge), sums, (s_main, s_main, s_edge)):
                    into[2 * m + k] = s * by if i == 0 else into[2 * m + k] + s * by
    for ch in range(6):
        force = straight[ch] + jnp.where(lane == 0, edge[ch], pltpu.roll(moved[ch], 1, axis=1))
        new = vel[ch] - weight[ch % 2] * force
        vel[ch] = new
        dis[ch] = at_left[ch, 1:17, :] + DT * new


def spread_kernel(stiff, entries, own, far):
    lane = lanes((24, COLS))
    for c in range(24):
        entries[24 * c : 24 * c + 24, :] = jnp.broadcast_to(stiff[:, c : c + 1], (24, COLS))
    for c, _, _, e in corners():
        if e == 0:
            on_left, on_right = [entries[24 * (c + 3 * n) : 24 * (c + 3 * n) + 24, :] for n in range(2)]
            own[24 * c : 24 * c + 24, :] = jnp.where(lane < 64, pltpu.roll(on_right, 21, axis=0), on_left)
            far[24 * c : 24 * c + 24, :] = jnp.where(lane < 64, pltpu.roll(on_left, 21, axis=0), on_right)


def look_up(table, owner, index, row, out):
    which = jnp.broadcast_to(index, (8, COLS))
    place, part = which & 127, (which >> 7) & 3
    found = None
    for c in range(4):
        got = jnp.take_along_axis(table[owner, 8 * c : 8 * c + 8, :], place, axis=1)
        found = got if found is None else jnp.where(part == c, got, found)
    found = jnp.where(which[0:4] >= 512, found[4:8], found[0:4])
    for c in range(4):
        out[c, row : row + 1, :] = found[c : c + 1]


def contact(words, points):
    depth = jnp.maximum(words[3] - (words[0] * points[0] + words[1] * points[1] + words[2] * points[2]), 0.0)
    return [words[m] * depth for m in range(3)]


def contact_kernel(who, table, index, vel, dis, weight, point, new_vel, new_dis, left, right, words, square):
    words[:, 8:16, :] = jnp.zeros((4, 8, COLS), F32)
    for b in range(ROWS + 2):
        look_up(table, who[0, ROWS - 1] if b == 0 else who[1, 0] if b == ROWS + 1 else who[2, b - 1], index[b : b + 1, :], b, words)
    pushes = contact([words[c] for c in range(4)], [point[m] for m in range(3)])
    for m in range(3):
        step = weight[0] * pushes[m]
        new_vel[2 * m] = (vel[2 * m] + step)[1:9]
        new_vel[2 * m + 1] = vel[2 * m + 1, 1:9, :]
        new_dis[2 * m] = dis[2 * m] + DT * step
        new_dis[2 * m + 1] = dis[2 * m + 1]
    for ch in range(6):
        square[16 * ch : 16 * ch + 16, :] = new_dis[ch]
    square[96:128, :] = jnp.zeros((32, COLS), F32)
    turned = jnp.transpose(square[...])
    left[...] = turned[0:1, :]
    right[...] = turned[COLS - 1 : COLS, :]


def inner_kernel(who, entries, own, table, pair, dis, vel, mass, ref, scale, base_dis, base_vel, weight, at_right, words):
    lane = lanes((ROWS, COLS))
    for b in range(ROWS):
        look_up(table, who[3, b], pair[1, b : b + 1, :], b, words)
    push = contact([words[c] for c in range(4)], [ref[m] + dis[2 * m, 1:9, :] for m in range(3)])
    for ch in range(6):
        at_right[ch] = pltpu.roll(dis[ch], COLS - 1, axis=1)
    straight = element_sums(by_corner(entries, 0), (dis, at_right), 1, scale.at[0], 0)
    moved = element_sums(by_corner(entries, 1), (dis, at_right), 1, scale.at[0], 0)
    edge = element_sums(by_corner(own, 0), (dis,), 1, scale.at[2], 0, ends=(0,))
    at_edge = (lane == 0) | (lane == COLS - 1)
    for k in range(2):
        weight[k] = DT / mass[k]
        for m in range(3):
            ch = 2 * m + k
            force = jnp.where(lane == COLS - 1, 0.0, straight[ch]) + jnp.where(lane == 0, 0.0, pltpu.roll(moved[ch], 1, axis=1))
            force = force + jnp.where(at_edge, edge[ch], 0.0)
            net = push[m] - force if k == 0 else -force
            new = vel[ch] + weight[k] * net
            base_vel[ch] = new
            base_dis[ch] = dis[ch, 1:9, :] + DT * new


def outer_kernel(base_dis, base_vel, weight, scale, far, from_left, from_right, out_dis, out_vel, side):
    edges = edge_columns(from_left[...], from_right[...])
    for ch in range(6):
        side[ch] = edges[16 * ch : 16 * ch + 16, :]
    forces = element_sums(by_corner(far, 0), (side,), 1, scale.at[2], 0, ends=(0,))
    lane = lanes((ROWS, COLS))
    for m in range(3):
        for k in range(2):
            ch = 2 * m + k
            change = weight[k] * jnp.where((lane == 0) | (lane == COLS - 1), forces[ch], 0.0)
            out_vel[m, k] = base_vel[ch] - change
            out_dis[m, k] = base_dis[ch] - DT * change


def call(kernel, outs, specs, scratch=(), room=16, out_specs=None, flops=1_000_000, moved=1_000_000):
    return pl.pallas_call(
        kernel,
        out_shape=outs,
        in_specs=specs,
        out_specs=out_specs or jax.tree.map(lambda _: VMEM, outs),
        scratch_shapes=list(scratch),
        compiler_params=pltpu.CompilerParams(vmem_limit_bytes=room << 20),
        cost_estimate=pl.CostEstimate(flops=flops, bytes_accessed=moved, transcendentals=0),
    )


def swapped(to_next, to_last, axis):
    size = lax.axis_size(axis)
    up = [(i, (i + 1) % size) for i in range(size)]
    down = [(j, i) for i, j in up]
    return lax.ppermute(to_next, axis, up), lax.ppermute(to_last, axis, down)


def shards(u, v, mass, mod, stiff, ref, facets, penalty, owners, pair):
    width = facets.shape[-1]
    owner = owners.reshape(2, 1, ROWS)
    sources = (facets.reshape(6 * width // COLS, COLS), penalty.reshape(width // COLS, COLS))
    table = call(
        table_kernel,
        struct(OWNERS, 32, COLS),
        [HBM] * 2,
        [pltpu.VMEM(x.shape, x.dtype) for x in sources]
        + [pltpu.VMEM((REPLICAS, 32, COLS), F32)]
        + [pltpu.SemaphoreType.DMA((n,)) for n in (2, OWNERS // REPLICAS)],
        room=60,
        out_specs=HBM,
    )(*sources)
    left, right = call(
        columns_kernel, (struct(1, COLS), struct(1, COLS)), [VMEM] * 2, [pltpu.VMEM((128, COLS), F32)]
    )(u, mod)
    tables = lax.all_to_all(table, "mesh", split_axis=0, concat_axis=0, tiled=True)
    from_left, from_right = swapped(right, left, "sub")
    up, down = call(pack_kernel, (struct(MSG, COLS), struct(MSG, COLS)), [VMEM] * 9)(
        u, v, mass, mod, ref, pair, owner, from_left, from_right
    )
    above, below = swapped(down, up, "mesh")
    entries, own, far = call(spread_kernel, (struct(576, COLS),) * 3, [VMEM])(stiff)
    vel, dis, weight, point, index, who, scale = call(
        first_kernel,
        (
            struct(6, 16, COLS),
            struct(6, 16, COLS),
            struct(2, 16, COLS),
            struct(3, 16, COLS),
            struct(16, COLS, dtype=jnp.int32),
            struct(8, COLS, dtype=jnp.int32),
            struct(3, 24, COLS),
        ),
        [VMEM] * 12,
        [pltpu.VMEM((8, 24, COLS), F32)] * 3,
    )(entries, owner, from_left, from_right, above, below, u, v, mass, mod, ref, pair)
    new_vel, new_dis, left, right = call(
        contact_kernel,
        (struct(6, ROWS, COLS), struct(6, 16, COLS), struct(1, COLS), struct(1, COLS)),
        [VMEM] * 7,
        [pltpu.VMEM((4, 16, COLS), F32), pltpu.VMEM((128, COLS), F32)],
    )(who, tables, index, vel, dis, weight, point)
    from_left, from_right = swapped(right, left, "sub")
    base_dis, base_vel, weight = call(
        inner_kernel,
        (struct(6, ROWS, COLS), struct(6, ROWS, COLS), struct(2, ROWS, COLS)),
        [VMEM] * 10,
        [pltpu.VMEM((6, 16, COLS), F32), pltpu.VMEM((4, 8, COLS), F32)],
    )(who, entries, own, tables, pair, new_dis, new_vel, mass, ref, scale)
    return call(
        outer_kernel,
        (struct(3, 2, ROWS, COLS), struct(3, 2, ROWS, COLS)),
        [VMEM] * 7,
        [pltpu.VMEM((6, 16, COLS), F32)],
    )(base_dis, base_vel, weight, scale, far, from_left, from_right)


def solution(mesh):
    in_specs = (
        P(None, None, "mesh", "sub"),
        P(None, None, "mesh", "sub"),
        P(None, "mesh", "sub"),
        P(None, "mesh", "sub"),
        P(),
        P(None, "mesh", "sub"),
        P("mesh", "sub", None, None),
        P("mesh", "sub", None),
        P(None, "mesh", "sub", None, None),
        P(None, "mesh", "sub"),
    )
    out_specs = (P(None, None, "mesh", "sub"), P(None, None, "mesh", "sub"))
    return jax.shard_map(shards, mesh=mesh, in_specs=in_specs, out_specs=out_specs, check_vma=False)
```

```python
import jax
import jax.numpy as jnp
from jax import lax
from jax.experimental import pallas as pl
from jax.experimental.pallas import tpu as pltpu
from jax.sharding import PartitionSpec as P

DT = 0.1
F32 = jnp.float32
VMEM = pl.BlockSpec(memory_space=pltpu.VMEM)
HBM = pl.BlockSpec(memory_space=pltpu.HBM)
ROWS = 8
COLS = 128
OWNERS = 32
REPLICAS = 8
AT_U, AT_E, AT_V, AT_M, AT_X, AT_P, AT_O, AT_L, AT_R = 0, 12, 16, 22, 24, 27, 28, 29, 30
MSG = 32


def struct(*shape, dtype=F32):
    return jax.ShapeDtypeStruct(shape, dtype)


def lanes(shape):
    return lax.broadcasted_iota(jnp.int32, shape, len(shape) - 1)


def table_kernel(fac, pen, table, fac_, pen_, mine, sems, out_sems):
    copies = [pltpu.make_async_copy(a, b, sems.at[n]) for n, (a, b) in enumerate(((fac, fac_), (pen, pen_)))]
    for copy in copies:
        copy.start()
    for copy in copies:
        copy.wait()
    root = jnp.sqrt(pen_[...])
    c, n = [[fac_[8 * (m + at) : 8 * (m + at) + 8, :] for m in range(3)] for at in (0, 3)]
    dist = n[0] * c[0] + n[1] * c[1] + n[2] * c[2]
    words = [root * n[0], root * n[1], root * n[2], root * dist]
    for q in range(4):
        tile = jnp.concatenate([w[4 * h + q : 4 * h + q + 1, :] for h in range(2) for w in words], axis=0)
        for r in range(REPLICAS):
            mine[r, 8 * q : 8 * q + 8, :] = tile
    outs = [pltpu.make_async_copy(mine, table.at[pl.ds(o * REPLICAS, REPLICAS)], out_sems.at[o]) for o in range(OWNERS // REPLICAS)]
    for copy in outs:
        copy.start()
    for copy in outs:
        copy.wait()


def columns_kernel(u, mod, left, right, square):
    for ch in range(8):
        square[16 * ch : 16 * ch + 8, :] = u[ch // 2, ch % 2] if ch < 6 else mod[ch - 6]
        square[16 * ch + 8 : 16 * ch + 16, :] = jnp.zeros((8, COLS), F32)
    turned = jnp.transpose(square[...])
    left[...] = turned[0:1, :]
    right[...] = turned[COLS - 1 : COLS, :]


def pack_kernel(odd, u, v, mass, mod, ref, pair, own, from_left, from_right, before, after, up, down):
    for out, two, one in ((down, ROWS - 2, ROWS - 1), (up, 0, 0)):
        for m in range(3):
            for k in range(2):
                ch = 2 * m + k
                out[AT_U + 2 * ch : AT_U + 2 * ch + 2, :] = u[m, k, two : two + 2, :]
                out[AT_V + ch : AT_V + ch + 1, :] = v[m, k, one : one + 1, :]
            out[AT_X + m : AT_X + m + 1, :] = ref[m, one : one + 1, :]
        for k in range(2):
            out[AT_E + 2 * k : AT_E + 2 * k + 2, :] = mod[k, two : two + 2, :]
            out[AT_M + k : AT_M + k + 1, :] = mass[k, one : one + 1, :]
        out[AT_P : AT_P + 1, :] = pair[0, one : one + 1, :].astype(F32)
        out[AT_O :, :] = jnp.zeros((MSG - AT_O, COLS), F32)
        out[AT_O : AT_O + 1, 0:ROWS] = own[0].astype(F32)
        out[AT_L : AT_L + 1, :] = from_left[...]
        out[AT_R : AT_R + 1, :] = from_right[...]
    here = odd[...] == 1
    before[...] = jnp.where(here, down[...], up[...])
    after[...] = jnp.where(here, up[...], down[...])


def extended(here, above, below):
    here, above, below = [jnp.broadcast_to(x, (8, COLS)) for x in (here, above, below)]
    at = lanes((8, COLS)) & 15
    out = jnp.where(at < 12, pltpu.roll(below, 10, axis=1), 0.0)
    out = jnp.where(at < 10, pltpu.roll(here, 2, axis=1), out)
    return jnp.where(at < 2, pltpu.roll(above, COLS - 6, axis=1), out)[0:1]


def edge_columns(from_left, from_right):
    sub = lax.broadcasted_iota(jnp.int32, (128, COLS), 0)
    both = jnp.where(sub < 64, jnp.broadcast_to(from_left, (128, COLS)), jnp.broadcast_to(from_right, (128, COLS)))
    return jnp.transpose(both)


def with_columns(here, edges):
    lane = lanes(here.shape)
    return jnp.where(lane == COLS - 1, edges, pltpu.roll(here, COLS - 1, axis=1))


def corners():
    return [(3 * (4 * k + 2 * x + e) + m, 2 * m + k, x, e) for k in range(2) for x in range(2) for e in range(2) for m in range(3)]


def element_sums(weight, rows_of, sides, scales, at, ends=(0, 1)):
    total = {}
    for i in range(2):
        start = at + 1 - i
        values = {c: rows_of[e][ch, pl.ds(start + x, ROWS), :] for c, ch, x, e in corners() if e in ends}
        for k in range(2):
            for m in range(3):
                force = None
                for c in values:
                    t = weight(k, i, m, c) * values[c]
                    force = t if force is None else force + t
                force = force * scales[pl.ds(start + sides, ROWS), :]
                total[2 * m + k] = force if i == 0 else total[2 * m + k] + force
    return [total[ch] for ch in range(6)]


def by_corner(entries, e):
    return lambda k, i, m, c: entries[entry(k, i, e, m, c), :]


def entry(k, i, e, m, c):
    at = 24 * c + 3 * (4 * k + 2 * i + e) + m
    return slice(at, at + 1)


def first_kernel(odd, entries, owner, from_left, from_right, before, after, u, v, mass, mod, ref, pair, vel, dis, weight, point, index, who, scale, at_left, at_right, at_edge, above, below):
    here = odd[...] == 1
    above[...] = jnp.where(here, after[...], before[...])
    below[...] = jnp.where(here, before[...], after[...])
    edges = edge_columns(
        extended(from_left[...], above[AT_L : AT_L + 1, :], below[AT_L : AT_L + 1, :]),
        extended(from_right[...], above[AT_R : AT_R + 1, :], below[AT_R : AT_R + 1, :]),
    )
    zero = jnp.zeros((8, COLS), F32)
    lane = lanes((16, COLS))
    for ch in range(8):
        at = AT_U + 2 * ch if ch < 6 else AT_E + 2 * (ch - 6)
        at_left[ch, 0:2, :] = above[at : at + 2, :]
        at_left[ch, 2:10, :] = u[ch // 2, ch % 2] if ch < 6 else mod[ch - 6]
        at_left[ch, 10:12, :] = below[at : at + 2, :]
        at_left[ch, 12:16, :] = zero[:4]
        side = edges[16 * ch : 16 * ch + 16, :]
        at_right[ch, 0:16, :] = with_columns(at_left[ch, 0:16, :], side)
        at_edge[ch, 0:16, :] = side
        for buf in (at_left, at_right, at_edge):
            buf[ch, 16:24, :] = zero
    here, right, side = [buf[6, 0:16, :] + buf[7, 0:16, :] for buf in (at_left, at_right, at_edge)]
    for n, both in enumerate((here + right, side + here)):
        scale[n, 0:16, :] = (both + pltpu.roll(both, 15, axis=0)) * 0.125
        scale[n, 16:24, :] = zero
    scale[2] = jnp.where(lanes((24, COLS)) < 64, scale[1], scale[0])
    for k in range(2):
        weight[k, 0:1, :] = above[AT_M + k : AT_M + k + 1, :]
        weight[k, 1:9, :] = mass[k]
        weight[k, 9:10, :] = below[AT_M + k : AT_M + k + 1, :]
        weight[k, 10:16, :] = jnp.ones((6, COLS), F32)
        weight[k] = DT / weight[k]
    for ch in range(6):
        vel[ch, 0:1, :] = above[AT_V + ch : AT_V + ch + 1, :]
        vel[ch, 1:9, :] = v[ch // 2, ch % 2]
        vel[ch, 9:10, :] = below[AT_V + ch : AT_V + ch + 1, :]
        vel[ch, 10:16, :] = zero[:6]
    for m in range(3):
        point[m, 0:1, :] = above[AT_X + m : AT_X + m + 1, :]
        point[m, 1:9, :] = ref[m]
        point[m, 9:10, :] = below[AT_X + m : AT_X + m + 1, :]
        point[m, 10:16, :] = zero[:6]
        point[m] = point[m] + at_left[2 * m, 1:17, :]
    index[0:1, :] = above[AT_P : AT_P + 1, :].astype(jnp.int32)
    index[1:9, :] = pair[0]
    index[9:10, :] = below[AT_P : AT_P + 1, :].astype(jnp.int32)
    index[10:16, :] = jnp.zeros((6, COLS), jnp.int32)
    who[...] = jnp.zeros((8, COLS), jnp.int32)
    who[0:1, :] = above[AT_O : AT_O + 1, :].astype(jnp.int32)
    who[1:2, :] = below[AT_O : AT_O + 1, :].astype(jnp.int32)
    for step in range(2):
        who[2 + step : 3 + step, 0:ROWS] = owner[step]
    straight, moved, edge = {}, {}, {}
    for i in range(2):
        start = 1 - i
        s_main, s_edge = [scale[n, start : start + 16, :] for n in range(2)]
        for k in range(2):
            for m in range(3):
                sums = [None, None, None]
                for c, ch, x, e in corners():
                    rows = slice(start + x, start + x + 16)
                    near = at_left[ch, rows, :]
                    main, side = (at_right[ch, rows, :], near) if e else (near, at_edge[ch, rows, :])
                    w0, w1 = [entries[entry(k, i, end, m, c), :] for end in range(2)]
                    terms = (w0 * main, w1 * main, w1 * side)
                    sums = [t if s is None else s + t for s, t in zip(sums, terms)]
                for into, s, by in zip((straight, moved, edge), sums, (s_main, s_main, s_edge)):
                    into[2 * m + k] = s * by if i == 0 else into[2 * m + k] + s * by
    for ch in range(6):
        force = straight[ch] + jnp.where(lane == 0, edge[ch], pltpu.roll(moved[ch], 1, axis=1))
        new = vel[ch] - weight[ch % 2] * force
        vel[ch] = new
        dis[ch] = at_left[ch, 1:17, :] + DT * new


def spread_kernel(stiff, entries, own, far):
    lane = lanes((24, COLS))
    for c in range(24):
        entries[24 * c : 24 * c + 24, :] = jnp.broadcast_to(stiff[:, c : c + 1], (24, COLS))
    for c, _, _, e in corners():
        if e == 0:
            on_left, on_right = [entries[24 * (c + 3 * n) : 24 * (c + 3 * n) + 24, :] for n in range(2)]
            own[24 * c : 24 * c + 24, :] = jnp.where(lane < 64, pltpu.roll(on_right, 21, axis=0), on_left)
            far[24 * c : 24 * c + 24, :] = jnp.where(lane < 64, pltpu.roll(on_left, 21, axis=0), on_right)


def look_up(table, owner, index, row, out):
    which = jnp.broadcast_to(index, (8, COLS))
    place, part = which & 127, (which >> 7) & 3
    found = None
    for c in range(4):
        got = jnp.take_along_axis(table[owner, 8 * c : 8 * c + 8, :], place, axis=1)
        found = got if found is None else jnp.where(part == c, got, found)
    found = jnp.where(which[0:4] >= 512, found[4:8], found[0:4])
    for c in range(4):
        out[c, row : row + 1, :] = found[c : c + 1]


def contact(words, points):
    depth = jnp.maximum(words[3] - (words[0] * points[0] + words[1] * points[1] + words[2] * points[2]), 0.0)
    return [words[m] * depth for m in range(3)]


def contact_kernel(who, table, index, vel, dis, weight, point, new_vel, new_dis, left, right, words, square):
    words[:, 8:16, :] = jnp.zeros((4, 8, COLS), F32)
    for b in range(ROWS + 2):
        look_up(table, who[0, ROWS - 1] if b == 0 else who[1, 0] if b == ROWS + 1 else who[2, b - 1], index[b : b + 1, :], b, words)
    pushes = contact([words[c] for c in range(4)], [point[m] for m in range(3)])
    for m in range(3):
        step = weight[0] * pushes[m]
        new_vel[2 * m] = (vel[2 * m] + step)[1:9]
        new_vel[2 * m + 1] = vel[2 * m + 1, 1:9, :]
        new_dis[2 * m] = dis[2 * m] + DT * step
        new_dis[2 * m + 1] = dis[2 * m + 1]
    for ch in range(6):
        square[16 * ch : 16 * ch + 16, :] = new_dis[ch]
    square[96:128, :] = jnp.zeros((32, COLS), F32)
    turned = jnp.transpose(square[...])
    left[...] = turned[0:1, :]
    right[...] = turned[COLS - 1 : COLS, :]


def inner_kernel(who, entries, own, table, pair, dis, vel, mass, ref, scale, base_dis, base_vel, weight, at_right, words):
    lane = lanes((ROWS, COLS))
    for b in range(ROWS):
        look_up(table, who[3, b], pair[1, b : b + 1, :], b, words)
    push = contact([words[c] for c in range(4)], [ref[m] + dis[2 * m, 1:9, :] for m in range(3)])
    for ch in range(6):
        at_right[ch] = pltpu.roll(dis[ch], COLS - 1, axis=1)
    straight = element_sums(by_corner(entries, 0), (dis, at_right), 1, scale.at[0], 0)
    moved = element_sums(by_corner(entries, 1), (dis, at_right), 1, scale.at[0], 0)
    edge = element_sums(by_corner(own, 0), (dis,), 1, scale.at[2], 0, ends=(0,))
    at_edge = (lane == 0) | (lane == COLS - 1)
    for k in range(2):
        weight[k] = DT / mass[k]
        for m in range(3):
            ch = 2 * m + k
            force = jnp.where(lane == COLS - 1, 0.0, straight[ch]) + jnp.where(lane == 0, 0.0, pltpu.roll(moved[ch], 1, axis=1))
            force = force + jnp.where(at_edge, edge[ch], 0.0)
            net = push[m] - force if k == 0 else -force
            new = vel[ch] + weight[k] * net
            base_vel[ch] = new
            base_dis[ch] = dis[ch, 1:9, :] + DT * new


def outer_kernel(base_dis, base_vel, weight, scale, far, from_left, from_right, out_dis, out_vel, side):
    edges = edge_columns(from_left[...], from_right[...])
    for ch in range(6):
        side[ch] = edges[16 * ch : 16 * ch + 16, :]
    forces = element_sums(by_corner(far, 0), (side,), 1, scale.at[2], 0, ends=(0,))
    lane = lanes((ROWS, COLS))
    for m in range(3):
        for k in range(2):
            ch = 2 * m + k
            change = weight[k] * jnp.where((lane == 0) | (lane == COLS - 1), forces[ch], 0.0)
            out_vel[m, k] = base_vel[ch] - change
            out_dis[m, k] = base_dis[ch] - DT * change


def call(kernel, outs, specs, scratch=(), room=16, out_specs=None, flops=1_000_000, moved=1_000_000):
    return pl.pallas_call(
        kernel,
        out_shape=outs,
        in_specs=specs,
        out_specs=out_specs or jax.tree.map(lambda _: VMEM, outs),
        scratch_shapes=list(scratch),
        compiler_params=pltpu.CompilerParams(vmem_limit_bytes=room << 20),
        cost_estimate=pl.CostEstimate(flops=flops, bytes_accessed=moved, transcendentals=0),
    )


def swapped(to_next, to_last, axis):
    size = lax.axis_size(axis)
    up = [(i, (i + 1) % size) for i in range(size)]
    down = [(j, i) for i, j in up]
    return lax.ppermute(to_next, axis, up), lax.ppermute(to_last, axis, down)


def paired(array, axis, start):
    size = lax.axis_size(axis)
    pairs = [(i, (i + 1) % size) for i in range(start, size, 2)]
    return lax.ppermute(array, axis, pairs + [(j, i) for i, j in pairs])


def shards(u, v, mass, mod, stiff, ref, facets, penalty, owners, pair):
    width = facets.shape[-1]
    owner = owners.reshape(2, 1, ROWS)
    sources = (facets.reshape(6 * width // COLS, COLS), penalty.reshape(width // COLS, COLS))
    table = call(
        table_kernel,
        struct(OWNERS, 32, COLS),
        [HBM] * 2,
        [pltpu.VMEM(x.shape, x.dtype) for x in sources]
        + [pltpu.VMEM((REPLICAS, 32, COLS), F32)]
        + [pltpu.SemaphoreType.DMA((n,)) for n in (2, OWNERS // REPLICAS)],
        room=60,
        out_specs=HBM,
    )(*sources)
    left, right = call(
        columns_kernel, (struct(1, COLS), struct(1, COLS)), [VMEM] * 2, [pltpu.VMEM((128, COLS), F32)]
    )(u, mod)
    tables = lax.all_to_all(table, "mesh", split_axis=0, concat_axis=0, tiled=True)
    from_left, from_right = swapped(right, left, "sub")
    rows = [pltpu.VMEM((MSG, COLS), F32)] * 2
    odd = jnp.full((1, COLS), lax.axis_index("mesh") % 2, jnp.int32)
    before, after = call(pack_kernel, (struct(MSG, COLS), struct(MSG, COLS)), [VMEM] * 10, rows)(
        odd, u, v, mass, mod, ref, pair, owner, from_left, from_right
    )
    before, after = paired(before, "mesh", 1), paired(after, "mesh", 0)
    entries, own, far = call(spread_kernel, (struct(576, COLS),) * 3, [VMEM])(stiff)
    vel, dis, weight, point, index, who, scale = call(
        first_kernel,
        (
            struct(6, 16, COLS),
            struct(6, 16, COLS),
            struct(2, 16, COLS),
            struct(3, 16, COLS),
            struct(16, COLS, dtype=jnp.int32),
            struct(8, COLS, dtype=jnp.int32),
            struct(3, 24, COLS),
        ),
        [VMEM] * 13,
        [pltpu.VMEM((8, 24, COLS), F32)] * 3 + rows,
    )(odd, entries, owner, from_left, from_right, before, after, u, v, mass, mod, ref, pair)
    new_vel, new_dis, left, right = call(
        contact_kernel,
        (struct(6, ROWS, COLS), struct(6, 16, COLS), struct(1, COLS), struct(1, COLS)),
        [VMEM] * 7,
        [pltpu.VMEM((4, 16, COLS), F32), pltpu.VMEM((128, COLS), F32)],
    )(who, tables, index, vel, dis, weight, point)
    from_left, from_right = swapped(right, left, "sub")
    base_dis, base_vel, weight = call(
        inner_kernel,
        (struct(6, ROWS, COLS), struct(6, ROWS, COLS), struct(2, ROWS, COLS)),
        [VMEM] * 10,
        [pltpu.VMEM((6, 16, COLS), F32), pltpu.VMEM((4, 8, COLS), F32)],
    )(who, entries, own, tables, pair, new_dis, new_vel, mass, ref, scale)
    return call(
        outer_kernel,
        (struct(3, 2, ROWS, COLS), struct(3, 2, ROWS, COLS)),
        [VMEM] * 7,
        [pltpu.VMEM((6, 16, COLS), F32)],
    )(base_dis, base_vel, weight, scale, far, from_left, from_right)


def solution(mesh):
    in_specs = (
        P(None, None, "mesh", "sub"),
        P(None, None, "mesh", "sub"),
        P(None, "mesh", "sub"),
        P(None, "mesh", "sub"),
        P(),
        P(None, "mesh", "sub"),
        P("mesh", "sub", None, None),
        P("mesh", "sub", None),
        P(None, "mesh", "sub", None, None),
        P(None, "mesh", "sub"),
    )
    out_specs = (P(None, None, "mesh", "sub"), P(None, None, "mesh", "sub"))
    return jax.shard_map(shards, mesh=mesh, in_specs=in_specs, out_specs=out_specs, check_vma=False)
```

```python
import jax
import jax.numpy as jnp
from jax import lax
from jax.experimental import pallas as pl
from jax.experimental.pallas import tpu as pltpu
from jax.sharding import PartitionSpec as P

DT = 0.1
F32 = jnp.float32
VMEM = pl.BlockSpec(memory_space=pltpu.VMEM)
HBM = pl.BlockSpec(memory_space=pltpu.HBM)
ROWS = 8
COLS = 128
OWNERS = 32
REPLICAS = 8
AT_U, AT_E, AT_V, AT_M, AT_X, AT_P, AT_O, AT_L, AT_R = 0, 12, 16, 22, 24, 27, 28, 29, 30
MSG = 32


def struct(*shape, dtype=F32):
    return jax.ShapeDtypeStruct(shape, dtype)


def lanes(shape):
    return lax.broadcasted_iota(jnp.int32, shape, len(shape) - 1)


def table_kernel(fac, pen, table, fac_, pen_, mine, sems, out_sems):
    copies = [pltpu.make_async_copy(a, b, sems.at[n]) for n, (a, b) in enumerate(((fac, fac_), (pen, pen_)))]
    for copy in copies:
        copy.start()
    for copy in copies:
        copy.wait()
    root = jnp.sqrt(pen_[...])
    c, n = [[fac_[8 * (m + at) : 8 * (m + at) + 8, :] for m in range(3)] for at in (0, 3)]
    dist = n[0] * c[0] + n[1] * c[1] + n[2] * c[2]
    words = [root * n[0], root * n[1], root * n[2], root * dist]
    for q in range(4):
        tile = jnp.concatenate([w[4 * h + q : 4 * h + q + 1, :] for h in range(2) for w in words], axis=0)
        for r in range(REPLICAS):
            mine[r, 8 * q : 8 * q + 8, :] = tile
    outs = [pltpu.make_async_copy(mine, table.at[pl.ds(o * REPLICAS, REPLICAS)], out_sems.at[o]) for o in range(OWNERS // REPLICAS)]
    for copy in outs:
        copy.start()
    for copy in outs:
        copy.wait()


def columns_kernel(u, mod, left, right, square):
    for ch in range(8):
        square[16 * ch : 16 * ch + 8, :] = u[ch // 2, ch % 2] if ch < 6 else mod[ch - 6]
        square[16 * ch + 8 : 16 * ch + 16, :] = jnp.zeros((8, COLS), F32)
    turned = jnp.transpose(square[...])
    left[...] = turned[0:1, :]
    right[...] = turned[COLS - 1 : COLS, :]


def pack_kernel(odd, u, v, mass, mod, ref, pair, own, from_left, from_right, before, after, up, down):
    for out, two, one in ((down, ROWS - 2, ROWS - 1), (up, 0, 0)):
        for m in range(3):
            for k in range(2):
                ch = 2 * m + k
                out[AT_U + 2 * ch : AT_U + 2 * ch + 2, :] = u[m, k, two : two + 2, :]
                out[AT_V + ch : AT_V + ch + 1, :] = v[m, k, one : one + 1, :]
            out[AT_X + m : AT_X + m + 1, :] = ref[m, one : one + 1, :]
        for k in range(2):
            out[AT_E + 2 * k : AT_E + 2 * k + 2, :] = mod[k, two : two + 2, :]
            out[AT_M + k : AT_M + k + 1, :] = mass[k, one : one + 1, :]
        out[AT_P : AT_P + 1, :] = pair[0, one : one + 1, :].astype(F32)
        out[AT_O :, :] = jnp.zeros((MSG - AT_O, COLS), F32)
        out[AT_O : AT_O + 1, 0:ROWS] = own[0].astype(F32)
        out[AT_L : AT_L + 1, :] = from_left[...]
        out[AT_R : AT_R + 1, :] = from_right[...]
    here = odd[...] == 1
    before[...] = jnp.where(here, down[...], up[...])
    after[...] = jnp.where(here, up[...], down[...])


def extended(here, above, below):
    here, above, below = [jnp.broadcast_to(x, (8, COLS)) for x in (here, above, below)]
    at = lanes((8, COLS)) & 15
    out = jnp.where(at < 12, pltpu.roll(below, 10, axis=1), 0.0)
    out = jnp.where(at < 10, pltpu.roll(here, 2, axis=1), out)
    return jnp.where(at < 2, pltpu.roll(above, COLS - 6, axis=1), out)[0:1]


def edge_columns(from_left, from_right):
    sub = lax.broadcasted_iota(jnp.int32, (128, COLS), 0)
    both = jnp.where(sub < 64, jnp.broadcast_to(from_left, (128, COLS)), jnp.broadcast_to(from_right, (128, COLS)))
    return jnp.transpose(both)


def with_columns(here, edges):
    lane = lanes(here.shape)
    return jnp.where(lane == COLS - 1, edges, pltpu.roll(here, COLS - 1, axis=1))


def corners():
    return [(3 * (4 * k + 2 * x + e) + m, 2 * m + k, x, e) for k in range(2) for x in range(2) for e in range(2) for m in range(3)]


def element_sums(weight, rows_of, sides, scales, at, ends=(0, 1)):
    total = {}
    for i in range(2):
        start = at + 1 - i
        values = {c: rows_of[e][ch, pl.ds(start + x, ROWS), :] for c, ch, x, e in corners() if e in ends}
        for k in range(2):
            for m in range(3):
                force = None
                for c in values:
                    t = weight(k, i, m, c) * values[c]
                    force = t if force is None else force + t
                force = force * scales[pl.ds(start + sides, ROWS), :]
                total[2 * m + k] = force if i == 0 else total[2 * m + k] + force
    return [total[ch] for ch in range(6)]


def by_corner(entries, e):
    return lambda k, i, m, c: entries[entry(k, i, e, m, c), :]


def entry(k, i, e, m, c):
    at = 24 * c + 3 * (4 * k + 2 * i + e) + m
    return slice(at, at + 1)


def first_kernel(odd, entries, owner, from_left, from_right, before, after, u, v, mass, mod, ref, pair, vel, dis, weight, point, index, who, scale, at_left, at_right, at_edge, above, below):
    here = odd[...] == 1
    above[...] = jnp.where(here, after[...], before[...])
    below[...] = jnp.where(here, before[...], after[...])
    edges = edge_columns(
        extended(from_left[...], above[AT_L : AT_L + 1, :], below[AT_L : AT_L + 1, :]),
        extended(from_right[...], above[AT_R : AT_R + 1, :], below[AT_R : AT_R + 1, :]),
    )
    zero = jnp.zeros((8, COLS), F32)
    lane = lanes((16, COLS))
    for ch in range(8):
        at = AT_U + 2 * ch if ch < 6 else AT_E + 2 * (ch - 6)
        at_left[ch, 0:2, :] = above[at : at + 2, :]
        at_left[ch, 2:10, :] = u[ch // 2, ch % 2] if ch < 6 else mod[ch - 6]
        at_left[ch, 10:12, :] = below[at : at + 2, :]
        at_left[ch, 12:16, :] = zero[:4]
        side = edges[16 * ch : 16 * ch + 16, :]
        at_right[ch, 0:16, :] = with_columns(at_left[ch, 0:16, :], side)
        at_edge[ch, 0:16, :] = side
        for buf in (at_left, at_right, at_edge):
            buf[ch, 16:24, :] = zero
    here, right, side = [buf[6, 0:16, :] + buf[7, 0:16, :] for buf in (at_left, at_right, at_edge)]
    for n, both in enumerate((here + right, side + here)):
        scale[n, 0:16, :] = (both + pltpu.roll(both, 15, axis=0)) * 0.125
        scale[n, 16:24, :] = zero
    scale[2] = jnp.where(lanes((24, COLS)) < 64, scale[1], scale[0])
    for k in range(2):
        weight[k, 0:1, :] = above[AT_M + k : AT_M + k + 1, :]
        weight[k, 1:9, :] = mass[k]
        weight[k, 9:10, :] = below[AT_M + k : AT_M + k + 1, :]
        weight[k, 10:16, :] = jnp.ones((6, COLS), F32)
        weight[k] = DT / weight[k]
    for ch in range(6):
        vel[ch, 0:1, :] = above[AT_V + ch : AT_V + ch + 1, :]
        vel[ch, 1:9, :] = v[ch // 2, ch % 2]
        vel[ch, 9:10, :] = below[AT_V + ch : AT_V + ch + 1, :]
        vel[ch, 10:16, :] = zero[:6]
    for m in range(3):
        point[m, 0:1, :] = above[AT_X + m : AT_X + m + 1, :]
        point[m, 1:9, :] = ref[m]
        point[m, 9:10, :] = below[AT_X + m : AT_X + m + 1, :]
        point[m, 10:16, :] = zero[:6]
        point[m] = point[m] + at_left[2 * m, 1:17, :]
    index[0:1, :] = above[AT_P : AT_P + 1, :].astype(jnp.int32)
    index[1:9, :] = pair[0]
    index[9:10, :] = below[AT_P : AT_P + 1, :].astype(jnp.int32)
    index[10:16, :] = jnp.zeros((6, COLS), jnp.int32)
    who[...] = jnp.zeros((8, COLS), jnp.int32)
    who[0:1, :] = above[AT_O : AT_O + 1, :].astype(jnp.int32)
    who[1:2, :] = below[AT_O : AT_O + 1, :].astype(jnp.int32)
    for step in range(2):
        who[2 + step : 3 + step, 0:ROWS] = owner[step]
    straight, moved, edge = {}, {}, {}
    for i in range(2):
        start = 1 - i
        s_main, s_edge = [scale[n, start : start + 16, :] for n in range(2)]
        for k in range(2):
            for m in range(3):
                sums = [None, None, None]
                for c, ch, x, e in corners():
                    rows = slice(start + x, start + x + 16)
                    near = at_left[ch, rows, :]
                    main, side = (at_right[ch, rows, :], near) if e else (near, at_edge[ch, rows, :])
                    w0, w1 = [entries[entry(k, i, end, m, c), :] for end in range(2)]
                    terms = (w0 * main, w1 * main, w1 * side)
                    sums = [t if s is None else s + t for s, t in zip(sums, terms)]
                for into, s, by in zip((straight, moved, edge), sums, (s_main, s_main, s_edge)):
                    into[2 * m + k] = s * by if i == 0 else into[2 * m + k] + s * by
    for ch in range(6):
        force = straight[ch] + jnp.where(lane == 0, edge[ch], pltpu.roll(moved[ch], 1, axis=1))
        new = vel[ch] - weight[ch % 2] * force
        vel[ch] = new
        dis[ch] = at_left[ch, 1:17, :] + DT * new


def spread_kernel(stiff, entries, own, far):
    lane = lanes((24, COLS))
    for c in range(24):
        entries[24 * c : 24 * c + 24, :] = jnp.broadcast_to(stiff[:, c : c + 1], (24, COLS))
    for c, _, _, e in corners():
        if e == 0:
            on_left, on_right = [entries[24 * (c + 3 * n) : 24 * (c + 3 * n) + 24, :] for n in range(2)]
            own[24 * c : 24 * c + 24, :] = jnp.where(lane < 64, pltpu.roll(on_right, 21, axis=0), on_left)
            far[24 * c : 24 * c + 24, :] = jnp.where(lane < 64, pltpu.roll(on_left, 21, axis=0), on_right)


def look_up(table, owner, index, row, out):
    which = jnp.broadcast_to(index, (8, COLS))
    place, part = which & 127, (which >> 7) & 3
    found = None
    for c in range(4):
        got = jnp.take_along_axis(table[owner, 8 * c : 8 * c + 8, :], place, axis=1)
        found = got if found is None else jnp.where(part == c, got, found)
    found = jnp.where(which[0:4] >= 512, found[4:8], found[0:4])
    for c in range(4):
        out[c, row : row + 1, :] = found[c : c + 1]


def contact(words, points):
    depth = jnp.maximum(words[3] - (words[0] * points[0] + words[1] * points[1] + words[2] * points[2]), 0.0)
    return [words[m] * depth for m in range(3)]


def contact_kernel(who, table, index, vel, dis, weight, point, new_vel, new_dis, left, right, words, square):
    words[:, 8:16, :] = jnp.zeros((4, 8, COLS), F32)
    for b in range(ROWS + 2):
        look_up(table, who[0, ROWS - 1] if b == 0 else who[1, 0] if b == ROWS + 1 else who[2, b - 1], index[b : b + 1, :], b, words)
    pushes = contact([words[c] for c in range(4)], [point[m] for m in range(3)])
    for m in range(3):
        step = weight[0] * pushes[m]
        new_vel[2 * m] = (vel[2 * m] + step)[1:9]
        new_vel[2 * m + 1] = vel[2 * m + 1, 1:9, :]
        new_dis[2 * m] = dis[2 * m] + DT * step
        new_dis[2 * m + 1] = dis[2 * m + 1]
    for ch in range(6):
        square[16 * ch : 16 * ch + 16, :] = new_dis[ch]
    square[96:128, :] = jnp.zeros((32, COLS), F32)
    turned = jnp.transpose(square[...])
    left[...] = turned[0:1, :]
    right[...] = turned[COLS - 1 : COLS, :]


def inner_kernel(who, entries, own, table, pair, dis, vel, mass, ref, scale, base_dis, base_vel, weight, at_right, words):
    lane = lanes((ROWS, COLS))
    for b in range(ROWS):
        look_up(table, who[3, b], pair[1, b : b + 1, :], b, words)
    push = contact([words[c] for c in range(4)], [ref[m] + dis[2 * m, 1:9, :] for m in range(3)])
    for ch in range(6):
        at_right[ch] = pltpu.roll(dis[ch], COLS - 1, axis=1)
    straight = element_sums(by_corner(entries, 0), (dis, at_right), 1, scale.at[0], 0)
    moved = element_sums(by_corner(entries, 1), (dis, at_right), 1, scale.at[0], 0)
    edge = element_sums(by_corner(own, 0), (dis,), 1, scale.at[2], 0, ends=(0,))
    at_edge = (lane == 0) | (lane == COLS - 1)
    for k in range(2):
        weight[k] = DT / mass[k]
        for m in range(3):
            ch = 2 * m + k
            force = jnp.where(lane == COLS - 1, 0.0, straight[ch]) + jnp.where(lane == 0, 0.0, pltpu.roll(moved[ch], 1, axis=1))
            force = force + jnp.where(at_edge, edge[ch], 0.0)
            net = push[m] - force if k == 0 else -force
            new = vel[ch] + weight[k] * net
            base_vel[ch] = new
            base_dis[ch] = dis[ch, 1:9, :] + DT * new


def outer_kernel(base_dis, base_vel, weight, scale, far, from_left, from_right, out_dis, out_vel, side, dis, vel, sems):
    edges = edge_columns(from_left[...], from_right[...])
    for ch in range(6):
        side[ch] = edges[16 * ch : 16 * ch + 16, :]
    forces = element_sums(by_corner(far, 0), (side,), 1, scale.at[2], 0, ends=(0,))
    lane = lanes((ROWS, COLS))
    copies = []
    for m in range(3):
        for k in range(2):
            ch = 2 * m + k
            change = weight[k] * jnp.where((lane == 0) | (lane == COLS - 1), forces[ch], 0.0)
            vel[m, k] = base_vel[ch] - change
            dis[m, k] = base_dis[ch] - DT * change
        copies += [pltpu.make_async_copy(a.at[m], b.at[m], sems.at[n, m]) for n, (a, b) in enumerate(((dis, out_dis), (vel, out_vel)))]
        for copy in copies[-2:]:
            copy.start()
    for copy in copies:
        copy.wait()


def call(kernel, outs, specs, scratch=(), room=16, out_specs=None, flops=1_000_000, moved=1_000_000):
    return pl.pallas_call(
        kernel,
        out_shape=outs,
        in_specs=specs,
        out_specs=out_specs or jax.tree.map(lambda _: VMEM, outs),
        scratch_shapes=list(scratch),
        compiler_params=pltpu.CompilerParams(vmem_limit_bytes=room << 20),
        cost_estimate=pl.CostEstimate(flops=flops, bytes_accessed=moved, transcendentals=0),
    )


def swapped(to_next, to_last, axis):
    size = lax.axis_size(axis)
    up = [(i, (i + 1) % size) for i in range(size)]
    down = [(j, i) for i, j in up]
    return lax.ppermute(to_next, axis, up), lax.ppermute(to_last, axis, down)


def paired(array, axis, start):
    size = lax.axis_size(axis)
    pairs = [(i, (i + 1) % size) for i in range(start, size, 2)]
    return lax.ppermute(array, axis, pairs + [(j, i) for i, j in pairs])


def shards(u, v, mass, mod, stiff, ref, facets, penalty, owners, pair):
    width = facets.shape[-1]
    owner = owners.reshape(2, 1, ROWS)
    sources = (facets.reshape(6 * width // COLS, COLS), penalty.reshape(width // COLS, COLS))
    table = call(
        table_kernel,
        struct(OWNERS, 32, COLS),
        [HBM] * 2,
        [pltpu.VMEM(x.shape, x.dtype) for x in sources]
        + [pltpu.VMEM((REPLICAS, 32, COLS), F32)]
        + [pltpu.SemaphoreType.DMA((n,)) for n in (2, OWNERS // REPLICAS)],
        room=60,
        out_specs=HBM,
    )(*sources)
    left, right = call(
        columns_kernel, (struct(1, COLS), struct(1, COLS)), [VMEM] * 2, [pltpu.VMEM((128, COLS), F32)]
    )(u, mod)
    tables = lax.all_to_all(table, "mesh", split_axis=0, concat_axis=0, tiled=True)
    from_left, from_right = swapped(right, left, "sub")
    rows = [pltpu.VMEM((MSG, COLS), F32)] * 2
    odd = jnp.full((1, COLS), lax.axis_index("mesh") % 2, jnp.int32)
    before, after = call(pack_kernel, (struct(MSG, COLS), struct(MSG, COLS)), [VMEM] * 10, rows)(
        odd, u, v, mass, mod, ref, pair, owner, from_left, from_right
    )
    before, after = paired(before, "mesh", 1), paired(after, "mesh", 0)
    entries, own, far = call(spread_kernel, (struct(576, COLS),) * 3, [VMEM])(stiff)
    vel, dis, weight, point, index, who, scale = call(
        first_kernel,
        (
            struct(6, 16, COLS),
            struct(6, 16, COLS),
            struct(2, 16, COLS),
            struct(3, 16, COLS),
            struct(16, COLS, dtype=jnp.int32),
            struct(8, COLS, dtype=jnp.int32),
            struct(3, 24, COLS),
        ),
        [VMEM] * 13,
        [pltpu.VMEM((8, 24, COLS), F32)] * 3 + rows,
    )(odd, entries, owner, from_left, from_right, before, after, u, v, mass, mod, ref, pair)
    new_vel, new_dis, left, right = call(
        contact_kernel,
        (struct(6, ROWS, COLS), struct(6, 16, COLS), struct(1, COLS), struct(1, COLS)),
        [VMEM] * 7,
        [pltpu.VMEM((4, 16, COLS), F32), pltpu.VMEM((128, COLS), F32)],
    )(who, tables, index, vel, dis, weight, point)
    from_left, from_right = swapped(right, left, "sub")
    base_dis, base_vel, weight = call(
        inner_kernel,
        (struct(6, ROWS, COLS), struct(6, ROWS, COLS), struct(2, ROWS, COLS)),
        [VMEM] * 10,
        [pltpu.VMEM((6, 16, COLS), F32), pltpu.VMEM((4, 8, COLS), F32)],
    )(who, entries, own, tables, pair, new_dis, new_vel, mass, ref, scale)
    return call(
        outer_kernel,
        (struct(3, 2, ROWS, COLS), struct(3, 2, ROWS, COLS)),
        [VMEM] * 7,
        [pltpu.VMEM((6, 16, COLS), F32)] + [pltpu.VMEM((3, 2, ROWS, COLS), F32)] * 2 + [pltpu.SemaphoreType.DMA((2, 3))],
        out_specs=(HBM, HBM),
    )(base_dis, base_vel, weight, scale, far, from_left, from_right)


def solution(mesh):
    in_specs = (
        P(None, None, "mesh", "sub"),
        P(None, None, "mesh", "sub"),
        P(None, "mesh", "sub"),
        P(None, "mesh", "sub"),
        P(),
        P(None, "mesh", "sub"),
        P("mesh", "sub", None, None),
        P("mesh", "sub", None),
        P(None, "mesh", "sub", None, None),
        P(None, "mesh", "sub"),
    )
    out_specs = (P(None, None, "mesh", "sub"), P(None, None, "mesh", "sub"))
    return jax.shard_map(shards, mesh=mesh, in_specs=in_specs, out_specs=out_specs, check_vma=False)
```
